32 devices in a mesh: tm: 8 (over y, x, core), space: 4 (over z).
Axes of the slice: x: 2, y: 2, z: 4, core: 2. Of those that a mesh axis runs over, the one named last changes fastest.
Arguments:
- eigen_vectors: bfloat16 [8, 2, 128, 3, 2048], P(None, None, 'tm', None, 'space'), may hold values from -90 to 90
- propagators: bfloat16 [8, 2, 128, 3, 2048], P('tm', None, None, None, 'space'), may hold values from -6 to 6
Outputs:
- perambulator: float32 [8, 128, 8, 2, 128], P(None, 'space', 'tm')
The draws below stay inside these ranges and needn't reach their ends.
All inputs are finite; a program needn't handle non-finite values.
Results may differ from the reference program's by a relative error of at most 0.0026.
Values may be sent and summed in bfloat16 or wider, within the bound.
No kernel may reach another device: no remote copies, remote signals or barrier semaphores. Data moves between devices by JAX's collectives and lax.ppermute only.
A program may use at most 64 MiB of HBM per device.

```python
import math
import jax
import jax.numpy as jnp
from jax import lax

NEV = 128
NCOL = 128
LS = 64
NT = 8
VOL = 2048


def draw_eigen_vectors(key, part):
    key = jax.random.fold_in(key, 11)
    key_main = jax.random.fold_in(key, 1)
    key_rough = jax.random.fold_in(key, 2)
    shape = (NT, 2, NEV, 3, VOL)
    position = jnp.arange(VOL, dtype=jnp.float32) / VOL
    rough = jax.random.uniform(key_rough, (1, 1, 1, 1, VOL), jnp.float32, 0.5, 1.5)
    values = jnp.clip(jax.random.normal(key_main, shape, jnp.float32), -4.0, 4.0)
    scale = jnp.power(10.0, position)
    return (values * scale * rough).astype(jnp.bfloat16)


def block_levels(key, shape, shards, low, top_value):
    level, own = 1.0, jax.random.fold_in(key, 6)
    for dim, shards_of in shards:
        steps = jnp.exp(jax.random.uniform(jax.random.fold_in(own, dim), (shards_of,), jnp.float32, low / len(shards), top_value / len(shards)))
        level = level * jnp.repeat(steps, shape[dim] // shards_of).reshape([-1 if axis == dim else 1 for axis in range(len(shape))])
    return level


def bell_draw(stream_key, extent, deviation, reach, pieces=(), kind=jnp.bfloat16):
    array = deviation * jax.random.normal(stream_key, extent, jnp.float32)
    if pieces:
        array = array * block_levels(stream_key, extent, pieces, -0.22, 0.18)
    return jnp.clip(array, -reach, reach).astype(kind)


def setup_inputs(seed: int = 0) -> dict:
    seeds = jax.random.split(jax.random.key(seed), 3)
    eigen_vectors = draw_eigen_vectors(jax.random.fold_in(seeds[2], 71), 0)
    propagators = bell_draw(seeds[1], (NT, 2, NCOL, 3, VOL), 1.0, 6.0, ((0, 8), (4, 4)))
    return dict(eigen_vectors=eigen_vectors, propagators=propagators)


momenta_table = ((0, 0, 0), (1, 0, 0), (0, 1, 0), (0, 0, 1), (1, 1, 0), (1, 0, 1), (0, 1, 1), (1, 1, 1))
epsilon_norm = 1e-06

def phase_tables(first_site, count, momentum):
    positions = first_site + jnp.arange(count, dtype=jnp.int32)
    coord_z = positions % LS
    coord_y = positions // LS % LS
    coord_x = positions // (LS * LS)
    wave = (momentum[0] * coord_x + momentum[1] * coord_y + momentum[2] * coord_z) % LS
    phase_angle = wave.astype(jnp.float32) * (2.0 * math.pi / LS)
    return (jnp.cos(phase_angle), jnp.sin(phase_angle))

def project(vectors, columns, cosine, sine):
    slices = vectors.shape[0]
    real_in = vectors[:, 0].astype(jnp.float32)
    imag_in = vectors[:, 1].astype(jnp.float32)
    w_real = (cosine * real_in - sine * imag_in).astype(jnp.bfloat16)
    w_imag = (-(sine * real_in + cosine * imag_in)).astype(jnp.bfloat16)
    left = jnp.stack([w_real, w_imag], 1)
    left = left.reshape(slices, 2, left.shape[2], -1).astype(jnp.float32)
    right = columns.reshape(slices, 2, columns.shape[2], -1).astype(jnp.float32)
    products = jnp.einsum('tcek,tdak->etcda', left, right)
    real_out = products[:, :, 0, 0] - products[:, :, 1, 1]
    imag_out = products[:, :, 0, 1] + products[:, :, 1, 0]
    return jnp.stack([real_out, imag_out], 2)

def reference(eigen_vectors, propagators):
    squares = lax.optimization_barrier(jnp.sum(jnp.square(eigen_vectors.astype(jnp.float32)), axis=(1, 3, 4)))
    inverse = lax.rsqrt(squares + epsilon_norm)
    results = []
    for momentum in momenta_table:
        cosine, sine = phase_tables(0, VOL, momentum)

        def one_slice(pair):
            return project(pair[0][None], pair[1][None], cosine, sine)[:, 0]
        sums = lax.map(one_slice, (eigen_vectors, propagators))
        scaled = sums * inverse[:, :, None, None]
        results.append(jnp.transpose(scaled, (1, 0, 2, 3)))
    return jnp.stack(results, 0)
```

```python
import functools
import math

import jax
import jax.numpy as jnp
import numpy as np
from jax import lax
from jax.experimental import pallas as pl
from jax.experimental.pallas import tpu as pltpu
from jax.sharding import PartitionSpec as P

LS = 64
LANES = 128

momenta_table = (
    (0, 0, 0),
    (1, 0, 0),
    (0, 1, 0),
    (0, 0, 1),
    (1, 1, 0),
    (1, 0, 1),
    (0, 1, 1),
    (1, 1, 1),
)
epsilon_norm = 1e-06


def window_waves(sites):
    positions = np.arange(sites)
    coords = np.stack([positions // (LS * LS), positions // LS % LS, positions % LS])
    return (np.asarray(momenta_table) @ coords) % LS


def distinct_rows(waves):
    rows, group = [], []
    for wave in waves:
        for known, row in enumerate(rows):
            if np.array_equal(row, wave):
                group.append(known)
                break
        else:
            group.append(len(rows))
            rows.append(wave)
    return np.stack(rows), tuple(group)


def trig_tables(waves):
    angle = waves.astype(np.float32) * np.float32(2.0 * math.pi / LS)
    return np.cos(angle).astype(np.float32), np.sin(angle).astype(np.float32)


def columns_kernel(p_ref, r_ref):
    cols, sites = p_ref.shape[2], p_ref.shape[3]
    for colour in range(p_ref.shape[1]):
        real = p_ref[0, colour].T
        imag = p_ref[1, colour].T
        r_ref[colour, :sites, :cols] = real
        r_ref[colour, :sites, cols:] = imag
        r_ref[colour, sites:, :cols] = -imag
        r_ref[colour, sites:, cols:] = real


def half_kernel(trivial, where_ref, tab_ref, r_ref, *refs):
    pieces = len(trivial[1])
    groups = len(trivial[0])
    v_refs, out_refs = refs[:pieces], refs[pieces : 2 * pieces]
    acc_ref, w_refs = refs[2 * pieces], refs[2 * pieces + 1 :]
    colours, rows, sites = v_refs[0].shape[1:]
    cols = r_ref.shape[2] // 2
    squares = [None] * pieces
    total = None
    for colour in range(colours):
        w_ref = w_refs[colour]
        for k, v_ref in enumerate(v_refs):
            real = v_ref[0, colour].astype(jnp.float32)
            imag = v_ref[1, colour].astype(jnp.float32)
            square = real * real + imag * imag
            square = sum(square[:, at : at + LANES] for at in range(0, sites, LANES))
            squares[k] = square if squares[k] is None else squares[k] + square
            for g in range(groups):
                at = (g * pieces + k) * rows
                if trivial[0][g]:
                    w_real, w_imag = real, -imag
                else:
                    cosine = tab_ref[2 * g : 2 * g + 1, :]
                    sine = tab_ref[2 * g + 1 : 2 * g + 2, :]
                    w_real = cosine * real - sine * imag
                    w_imag = -(sine * real + cosine * imag)
                w_ref[at : at + rows, :sites] = w_real.astype(jnp.bfloat16)
                w_ref[at : at + rows, sites:] = w_imag.astype(jnp.bfloat16)
        part = jnp.dot(w_ref[...], r_ref[colour], preferred_element_type=jnp.float32)
        total = part if total is None else total + part
    acc_ref[: groups * pieces * rows, :cols] = total[:, :cols]
    acc_ref[: groups * pieces * rows, cols:] = total[:, cols:]
    lane = lax.broadcasted_iota(jnp.int32, (rows, LANES), 1)
    for k in range(pieces):
        whole = jnp.broadcast_to(jnp.sum(squares[k], axis=1, keepdims=True), (rows, LANES))
        high = whole.astype(jnp.bfloat16).astype(jnp.float32)
        at = (groups * pieces + k) * rows
        acc_ref[at : at + rows, :LANES] = jnp.where(lane < LANES // 2, high, whole - high)
    for q in range(pieces):
        k = jnp.bitwise_xor(where_ref[0], q)
        out_ref = out_refs[q]
        for g in range(groups):
            at = pl.multiple_of((g * pieces + k) * rows, rows)
            for part in range(2):
                out_ref[2 * g + part] = acc_ref[
                    pl.ds(at, rows), part * cols : (part + 1) * cols
                ].astype(out_ref.dtype)
        at = pl.multiple_of((groups * pieces + k) * rows, rows)
        out_ref[2 * groups] = acc_ref[pl.ds(at, rows), :LANES].astype(out_ref.dtype)


def finish_kernel(group, core_ref, *refs):
    out_ref = refs[-1]
    per_half = (len(refs) - 1) // 2
    tiles, rows, cols = refs[0].shape
    for half in range(2):
        parts = refs[half * per_half : (half + 1) * per_half]
        first = pl.multiple_of(jnp.bitwise_xor(core_ref[0], half) * (2 * rows), 2 * rows)

        def summed(tile):
            value = parts[0][tile].astype(jnp.float32)
            for ref in parts[1:]:
                value = value + ref[tile].astype(jnp.float32)
            return value

        both = summed(tiles - 1)
        squares = both[:, :1] + both[:, LANES // 2 : LANES // 2 + 1]
        inverse = lax.rsqrt(squares + epsilon_norm)
        for g in range((tiles - 1) // 2):
            for part in range(2):
                value = summed(2 * g + part) * inverse
                for m, mine in enumerate(group):
                    if mine == g:
                        at = m * 4 * rows + first + part
                        out_ref[pl.ds(at, rows, stride=2), :] = value


def in_vmem(count):
    return [pl.BlockSpec(memory_space=pltpu.VMEM)] * count


def scalar():
    return [pl.BlockSpec(memory_space=pltpu.SMEM)]


def per_device_permutes(eigen_vectors, propagators):
    tm, space = lax.axis_size("tm"), lax.axis_size("space")
    me, z = lax.axis_index("tm"), lax.axis_index("space")
    rows, sites = eigen_vectors.shape[2], eigen_vectors.shape[4]
    cols = propagators.shape[2]
    waves, group = distinct_rows(window_waves(sites * space))
    groups = len(waves)
    trivial = tuple(not wave.any() for wave in waves)
    cosine, sine = trig_tables(waves)
    tables = np.stack([cosine, sine], 1).reshape(2 * groups, space, sites).transpose(1, 0, 2)
    table = lax.dynamic_index_in_dim(jnp.asarray(tables), z, 0, keepdims=False)

    vectors = jnp.transpose(eigen_vectors, (0, 1, 3, 2, 4))
    columns = jnp.transpose(propagators[0], (0, 2, 1, 3))
    colours = vectors.shape[2]

    def piece(r):
        mine = lax.dynamic_index_in_dim(vectors, jnp.bitwise_xor(me, r), 0, keepdims=False)
        if r == 0:
            return mine
        return lax.ppermute(mine, "tm", [(i, i ^ r) for i in range(tm)])

    right = pl.pallas_call(
        columns_kernel,
        out_shape=jax.ShapeDtypeStruct((colours, 2 * sites, 2 * cols), jnp.bfloat16),
        in_specs=in_vmem(1),
        out_specs=in_vmem(1)[0],
        cost_estimate=pl.CostEstimate(flops=0, bytes_accessed=3 * 2**20, transcendentals=0),
        compiler_params=pltpu.CompilerParams(vmem_limit_bytes=16 * 2**20),
    )(columns)

    where = jnp.bitwise_xor(me // 2, z).astype(jnp.int32).reshape(1)
    core = (me % 2).astype(jnp.int32).reshape(1)
    tiles = 2 * groups + 1
    out_tile = lambda dtype: jax.ShapeDtypeStruct((tiles, rows, cols), dtype)
    half = pl.pallas_call(
        functools.partial(half_kernel, (trivial, (None,) * space)),
        out_shape=[out_tile(jnp.float32)] + [out_tile(jnp.bfloat16)] * (space - 1),
        in_specs=scalar() + in_vmem(2 + space),
        out_specs=in_vmem(space),
        scratch_shapes=[pltpu.VMEM(((groups + 1) * space * rows, 2 * cols), jnp.float32)]
        + [pltpu.VMEM((groups * space * rows, 2 * sites), jnp.bfloat16)] * colours,
        cost_estimate=pl.CostEstimate(
            flops=2 * groups * space * rows * colours * 2 * sites * 2 * cols,
            bytes_accessed=2 * 2**20,
            transcendentals=0,
        ),
        compiler_params=pltpu.CompilerParams(vmem_limit_bytes=24 * 2**20),
    )
    sent = [[piece(r) for r in range(first, tm, 2)] for first in range(2)]
    parts = []
    for pieces in sent:
        own, *others = half(where, table, right, *pieces)
        parts.append(own)
        for q, other in enumerate(others, 1):
            parts.append(lax.ppermute(other, "space", [(i, i ^ q) for i in range(space)]))
    out = pl.pallas_call(
        functools.partial(finish_kernel, group),
        out_shape=jax.ShapeDtypeStruct((len(group) * 2 * rows * 2, cols), jnp.float32),
        in_specs=scalar() + in_vmem(len(parts)),
        out_specs=in_vmem(1)[0],
        cost_estimate=pl.CostEstimate(flops=2**20, bytes_accessed=2**20, transcendentals=0),
        compiler_params=pltpu.CompilerParams(vmem_limit_bytes=16 * 2**20),
    )(core, *parts)
    return out.reshape(len(group), 2 * rows, 1, 2, cols)


def project(vectors, columns, cosine, sine):
    slices = vectors.shape[0]
    real_in = vectors[:, 0].astype(jnp.float32)
    imag_in = vectors[:, 1].astype(jnp.float32)
    w_real = (cosine * real_in - sine * imag_in).astype(jnp.bfloat16)
    w_imag = (-(sine * real_in + cosine * imag_in)).astype(jnp.bfloat16)
    left = jnp.stack([w_real, w_imag], 1)
    left = left.reshape(slices, 2, left.shape[2], -1)
    right = columns.reshape(slices, 2, columns.shape[2], -1)
    products = jnp.einsum("tcek,tdak->etcda", left, right, preferred_element_type=jnp.float32)
    real_out = products[:, :, 0, 0] - products[:, :, 1, 1]
    imag_out = products[:, :, 0, 1] + products[:, :, 1, 0]
    return jnp.stack([real_out, imag_out], 2)


def per_device_general(eigen_vectors, propagators):
    vectors = lax.all_to_all(eigen_vectors, "tm", split_axis=0, concat_axis=2, tiled=True)
    sites = vectors.shape[4]
    space = lax.axis_size("space")
    rows = vectors.shape[2] // space
    z = lax.axis_index("space")
    squares = lax.psum(jnp.sum(jnp.square(vectors.astype(jnp.float32)), axis=(1, 3, 4)), "space")
    inverse = lax.rsqrt(squares + epsilon_norm)
    mine = lax.dynamic_slice_in_dim(inverse, z * rows, rows, 1)
    row_scale = jnp.transpose(mine)[:, :, None, None]
    waves, group = distinct_rows(window_waves(sites * space))
    positions = z * sites + jnp.arange(sites, dtype=jnp.int32)
    coords = (positions // (LS * LS), positions // LS % LS, positions % LS)
    results = []
    for g in range(len(waves)):
        momentum = momenta_table[group.index(g)]
        wave = sum(n * x for n, x in zip(momentum, coords)) % LS
        angle = wave.astype(jnp.float32) * (2.0 * math.pi / LS)
        sums = project(vectors, propagators, jnp.cos(angle), jnp.sin(angle))
        sums = lax.psum_scatter(sums, "space", scatter_dimension=0, tiled=True)
        results.append(sums * row_scale)
    return jnp.stack([results[g] for g in group], 0)


def solution(mesh):
    tm, space = mesh.shape["tm"], mesh.shape["space"]

    def per_device(eigen_vectors, propagators):
        rows, sites = eigen_vectors.shape[2], eigen_vectors.shape[4]
        fits = (
            tm == 2 * space
            and space & (space - 1) == 0
            and eigen_vectors.shape[0] == tm
            and rows % 16 == 0
            and sites % LANES == 0
            and propagators.shape[2] == LANES
        )
        form = per_device_permutes if fits else per_device_general
        return form(eigen_vectors, propagators)

    placed = (P(None, None, "tm", None, "space"), P("tm", None, None, None, "space"))
    return jax.shard_map(
        per_device,
        mesh=mesh,
        in_specs=placed,
        out_specs=P(None, "space", "tm", None, None),
        check_vma=False,
    )
```

```python
import functools
import math

import jax
import jax.numpy as jnp
import numpy as np
from jax import lax
from jax.experimental import pallas as pl
from jax.experimental.pallas import tpu as pltpu
from jax.sharding import PartitionSpec as P

LS = 64
LANES = 128

momenta_table = (
    (0, 0, 0),
    (1, 0, 0),
    (0, 1, 0),
    (0, 0, 1),
    (1, 1, 0),
    (1, 0, 1),
    (0, 1, 1),
    (1, 1, 1),
)
epsilon_norm = 1e-06


def window_waves(sites):
    positions = np.arange(sites)
    coords = np.stack([positions // (LS * LS), positions // LS % LS, positions % LS])
    return (np.asarray(momenta_table) @ coords) % LS


def distinct_rows(waves):
    rows, group = [], []
    for wave in waves:
        for known, row in enumerate(rows):
            if np.array_equal(row, wave):
                group.append(known)
                break
        else:
            group.append(len(rows))
            rows.append(wave)
    return np.stack(rows), tuple(group)


def trig_tables(waves):
    angle = waves.astype(np.float32) * np.float32(2.0 * math.pi / LS)
    return np.cos(angle).astype(np.float32), np.sin(angle).astype(np.float32)


def project_rows(trivial, v_refs, tab_ref, right, w_refs):
    pieces, groups = len(v_refs), len(trivial)
    colours, rows, sites = v_refs[0].shape[1:]
    squares = [None] * pieces
    total = None
    for colour in range(colours):
        w_ref = w_refs[colour]
        for k, v_ref in enumerate(v_refs):
            real = v_ref[0, colour].astype(jnp.float32)
            imag = v_ref[1, colour].astype(jnp.float32)
            square = real * real + imag * imag
            square = sum(square[:, at : at + LANES] for at in range(0, sites, LANES))
            squares[k] = square if squares[k] is None else squares[k] + square
            for g in range(groups):
                at = (g * pieces + k) * rows
                if trivial[g]:
                    w_real, w_imag = real, -imag
                else:
                    cosine = tab_ref[2 * g : 2 * g + 1, :]
                    sine = tab_ref[2 * g + 1 : 2 * g + 2, :]
                    w_real = cosine * real - sine * imag
                    w_imag = -(sine * real + cosine * imag)
                w_ref[at : at + rows, :sites] = w_real.astype(jnp.bfloat16)
                w_ref[at : at + rows, sites:] = w_imag.astype(jnp.bfloat16)
        part = jnp.dot(w_ref[...], right(colour), preferred_element_type=jnp.float32)
        total = part if total is None else total + part
    return total, squares


def square_tile(square):
    whole = jnp.broadcast_to(jnp.sum(square, axis=1, keepdims=True), square.shape)
    high = whole.astype(jnp.bfloat16).astype(jnp.float32)
    lane = lax.broadcasted_iota(jnp.int32, square.shape, 1)
    return jnp.where(lane < LANES // 2, high, whole - high)


def first_kernel(trivial, tab_ref, p_ref, *refs):
    v_refs, r_ref, out_refs, w_refs = refs[:2], refs[2], refs[3:5], refs[5:]
    cols, sites = p_ref.shape[2], p_ref.shape[3]
    rows = v_refs[0].shape[2]
    for colour in range(p_ref.shape[1]):
        real = p_ref[0, colour].T
        imag = p_ref[1, colour].T
        r_ref[colour, :sites, :cols] = real
        r_ref[colour, :sites, cols:] = imag
        r_ref[colour, sites:, :cols] = -imag
        r_ref[colour, sites:, cols:] = real
    total, squares = project_rows(trivial, v_refs, tab_ref, lambda colour: r_ref[colour], w_refs)
    for k, out_ref in enumerate(out_refs):
        for g in range(len(trivial)):
            at = (2 * g + k) * rows
            for part in range(2):
                out_ref[2 * g + part] = total[at : at + rows, part * cols : (part + 1) * cols]
        out_ref[2 * len(trivial)] = square_tile(squares[k])


def rows_kernel(trivial, where_ref, tab_ref, r_ref, own_ref, sibling_ref, *refs):
    owners = 4
    v_refs, refs = refs[: 2 * (owners - 1)], refs[2 * (owners - 1) :]
    out_refs, acc_ref, w_refs = refs[:owners], refs[owners], refs[owners + 1 :]
    tiles, rows, cols = own_ref.shape
    total, squares = project_rows(trivial, v_refs, tab_ref, lambda colour: r_ref[colour], w_refs)
    acc_ref[0, :, :rows] = own_ref[...]
    acc_ref[0, :, rows:] = sibling_ref[...]
    for n in range(len(v_refs)):
        owner, at = divmod(n + 2, 2)
        for g in range(len(trivial)):
            low = (g * len(v_refs) + n) * rows
            for part in range(2):
                acc_ref[owner, 2 * g + part, at * rows : (at + 1) * rows] = total[
                    low : low + rows, part * cols : (part + 1) * cols
                ]
        acc_ref[owner, tiles - 1, at * rows : (at + 1) * rows] = square_tile(squares[n])
    for q, out_ref in enumerate(out_refs):
        out_ref[...] = acc_ref[jnp.bitwise_xor(where_ref[0], q)].astype(out_ref.dtype)


def finish_kernel(group, core_ref, *refs):
    parts, out_ref = refs[:-1], refs[-1]
    tiles, rows, cols = refs[0].shape
    rows //= 2

    def summed(tile, at):
        value = parts[0][tile, at : at + rows].astype(jnp.float32)
        for ref in parts[1:]:
            value = value + ref[tile, at : at + rows].astype(jnp.float32)
        return value

    for other in range(2):
        first = pl.multiple_of(jnp.bitwise_xor(core_ref[0], other) * (2 * rows), 2 * rows)
        both = summed(tiles - 1, other * rows)
        squares = both[:, :1] + both[:, LANES // 2 : LANES // 2 + 1]
        inverse = lax.rsqrt(squares + epsilon_norm)
        for g in range((tiles - 1) // 2):
            for part in range(2):
                value = summed(2 * g + part, other * rows) * inverse
                for m, mine in enumerate(group):
                    if mine == g:
                        at = m * 4 * rows + first + part
                        out_ref[pl.ds(at, rows, stride=2), :] = value


def in_vmem(count):
    return [pl.BlockSpec(memory_space=pltpu.VMEM)] * count


def scalar():
    return [pl.BlockSpec(memory_space=pltpu.SMEM)]


def per_device_permutes(eigen_vectors, propagators):
    tm, space = lax.axis_size("tm"), lax.axis_size("space")
    me, z = lax.axis_index("tm"), lax.axis_index("space")
    rows, sites = eigen_vectors.shape[2], eigen_vectors.shape[4]
    cols = propagators.shape[2]
    waves, group = distinct_rows(window_waves(sites * space))
    groups = len(waves)
    trivial = tuple(not wave.any() for wave in waves)
    cosine, sine = trig_tables(waves)
    tables = np.stack([cosine, sine], 1).reshape(2 * groups, space, sites).transpose(1, 0, 2)
    table = lax.dynamic_index_in_dim(jnp.asarray(tables), z, 0, keepdims=False)

    vectors = jnp.transpose(eigen_vectors, (0, 1, 3, 2, 4))
    columns = jnp.transpose(propagators[0], (0, 2, 1, 3))
    colours = vectors.shape[2]

    def piece(source, r):
        return lax.dynamic_index_in_dim(source, jnp.bitwise_xor(me, r), 0, keepdims=False)

    def swapped(mine, r):
        return lax.ppermute(mine, "tm", [(i, i ^ r) for i in range(tm)])

    tiles = 2 * groups + 1
    tile = lambda dtype, count: jax.ShapeDtypeStruct((tiles, count * rows, cols), dtype)
    w_scratch = lambda count: [pltpu.VMEM((groups * count * rows, 2 * sites), jnp.bfloat16)] * colours
    small = pl.CostEstimate(flops=2**20, bytes_accessed=2**20, transcendentals=0)
    params = pltpu.CompilerParams(vmem_limit_bytes=24 * 2**20)

    order = (2, 4, 6, 3, 5, 7)
    far = {r: piece(vectors, r) for r in order[:3]}
    vectors, far = lax.optimization_barrier((vectors, far))
    own, sibling = piece(vectors, 0), piece(vectors, 1)
    far.update({r: piece(vectors, r) for r in order[3:]})
    far = {r: swapped(far[r], r) for r in order}
    sibling = swapped(sibling, 1)

    right, own_sums, sibling_sums = pl.pallas_call(
        functools.partial(first_kernel, trivial),
        out_shape=[jax.ShapeDtypeStruct((colours, 2 * sites, 2 * cols), jnp.bfloat16)]
        + [tile(jnp.float32, 1)] * 2,
        in_specs=in_vmem(4),
        out_specs=in_vmem(3),
        scratch_shapes=w_scratch(2),
        cost_estimate=small,
        compiler_params=params,
    )(table, columns, own, sibling)

    where = jnp.bitwise_xor(me // 2, z).astype(jnp.int32).reshape(1)
    core = (me % 2).astype(jnp.int32).reshape(1)
    own, *others = pl.pallas_call(
        functools.partial(rows_kernel, trivial),
        out_shape=[tile(jnp.float32, 2)] + [tile(jnp.bfloat16, 2)] * (space - 1),
        in_specs=scalar() + in_vmem(4 + len(far)),
        out_specs=in_vmem(space),
        scratch_shapes=[pltpu.VMEM((space, tiles, 2 * rows, cols), jnp.float32)] + w_scratch(len(far)),
        cost_estimate=small,
        compiler_params=params,
    )(where, table, right, own_sums, sibling_sums, *[far[r] for r in range(2, tm)])
    parts = [own]
    for q in (2, 3, 1):
        parts.append(lax.ppermute(others[q - 1], "space", [(i, i ^ q) for i in range(space)]))
    out = pl.pallas_call(
        functools.partial(finish_kernel, group),
        out_shape=jax.ShapeDtypeStruct((len(group) * 2 * rows * 2, cols), jnp.float32),
        in_specs=scalar() + in_vmem(len(parts)),
        out_specs=in_vmem(1)[0],
        cost_estimate=small,
        compiler_params=params,
    )(core, *parts)
    return out.reshape(len(group), 2 * rows, 1, 2, cols)


def project(vectors, columns, cosine, sine):
    slices = vectors.shape[0]
    real_in = vectors[:, 0].astype(jnp.float32)
    imag_in = vectors[:, 1].astype(jnp.float32)
    w_real = (cosine * real_in - sine * imag_in).astype(jnp.bfloat16)
    w_imag = (-(sine * real_in + cosine * imag_in)).astype(jnp.bfloat16)
    left = jnp.stack([w_real, w_imag], 1)
    left = left.reshape(slices, 2, left.shape[2], -1)
    right = columns.reshape(slices, 2, columns.shape[2], -1)
    products = jnp.einsum("tcek,tdak->etcda", left, right, preferred_element_type=jnp.float32)
    real_out = products[:, :, 0, 0] - products[:, :, 1, 1]
    imag_out = products[:, :, 0, 1] + products[:, :, 1, 0]
    return jnp.stack([real_out, imag_out], 2)


def per_device_general(eigen_vectors, propagators):
    vectors = lax.all_to_all(eigen_vectors, "tm", split_axis=0, concat_axis=2, tiled=True)
    sites = vectors.shape[4]
    space = lax.axis_size("space")
    rows = vectors.shape[2] // space
    z = lax.axis_index("space")
    squares = lax.psum(jnp.sum(jnp.square(vectors.astype(jnp.float32)), axis=(1, 3, 4)), "space")
    inverse = lax.rsqrt(squares + epsilon_norm)
    mine = lax.dynamic_slice_in_dim(inverse, z * rows, rows, 1)
    row_scale = jnp.transpose(mine)[:, :, None, None]
    waves, group = distinct_rows(window_waves(sites * space))
    positions = z * sites + jnp.arange(sites, dtype=jnp.int32)
    coords = (positions // (LS * LS), positions // LS % LS, positions % LS)
    results = []
    for g in range(len(waves)):
        momentum = momenta_table[group.index(g)]
        wave = sum(n * x for n, x in zip(momentum, coords)) % LS
        angle = wave.astype(jnp.float32) * (2.0 * math.pi / LS)
        sums = project(vectors, propagators, jnp.cos(angle), jnp.sin(angle))
        sums = lax.psum_scatter(sums, "space", scatter_dimension=0, tiled=True)
        results.append(sums * row_scale)
    return jnp.stack([results[g] for g in group], 0)


def solution(mesh):
    tm, space = mesh.shape["tm"], mesh.shape["space"]

    def per_device(eigen_vectors, propagators):
        rows, sites = eigen_vectors.shape[2], eigen_vectors.shape[4]
        fits = (
            tm == 8
            and space == 4
            and eigen_vectors.shape[0] == tm
            and rows % 16 == 0
            and sites % LANES == 0
            and propagators.shape[2] == LANES
        )
        form = per_device_permutes if fits else per_device_general
        return form(eigen_vectors, propagators)

    placed = (P(None, None, "tm", None, "space"), P("tm", None, None, None, "space"))
    return jax.shard_map(
        per_device,
        mesh=mesh,
        in_specs=placed,
        out_specs=P(None, "space", "tm", None, None),
        check_vma=False,
    )
```

```python
import functools
import math

import jax
import jax.numpy as jnp
import numpy as np
from jax import lax
from jax.experimental import pallas as pl
from jax.experimental.pallas import tpu as pltpu
from jax.sharding import PartitionSpec as P

LS = 64
LANES = 128

momenta_table = (
    (0, 0, 0),
    (1, 0, 0),
    (0, 1, 0),
    (0, 0, 1),
    (1, 1, 0),
    (1, 0, 1),
    (0, 1, 1),
    (1, 1, 1),
)
epsilon_norm = 1e-06


def window_waves(sites):
    positions = np.arange(sites)
    coords = np.stack([positions // (LS * LS), positions // LS % LS, positions % LS])
    return (np.asarray(momenta_table) @ coords) % LS


def distinct_rows(waves):
    rows, group = [], []
    for wave in waves:
        for known, row in enumerate(rows):
            if np.array_equal(row, wave):
                group.append(known)
                break
        else:
            group.append(len(rows))
            rows.append(wave)
    return np.stack(rows), tuple(group)


def trig_tables(waves):
    angle = waves.astype(np.float32) * np.float32(2.0 * math.pi / LS)
    return np.cos(angle).astype(np.float32), np.sin(angle).astype(np.float32)


def project_rows(trivial, v_refs, tab_ref, right, w_refs):
    pieces, groups = len(v_refs), len(trivial)
    colours, rows, sites = v_refs[0].shape[-3:]
    squares = [None] * pieces
    total = None
    for colour in range(colours):
        w_ref = w_refs[colour]
        for k, v_ref in enumerate(v_refs):
            real = v_ref[0, colour].astype(jnp.float32)
            imag = v_ref[1, colour].astype(jnp.float32)
            square = real * real + imag * imag
            square = sum(square[:, at : at + LANES] for at in range(0, sites, LANES))
            squares[k] = square if squares[k] is None else squares[k] + square
            for g in range(groups):
                at = (g * pieces + k) * rows
                if trivial[g]:
                    w_real, w_imag = real, -imag
                else:
                    cosine = tab_ref[2 * g : 2 * g + 1, :]
                    sine = tab_ref[2 * g + 1 : 2 * g + 2, :]
                    w_real = cosine * real - sine * imag
                    w_imag = -(sine * real + cosine * imag)
                w_ref[at : at + rows, :sites] = w_real.astype(jnp.bfloat16)
                w_ref[at : at + rows, sites:] = w_imag.astype(jnp.bfloat16)
        part = jnp.dot(w_ref[...], right(colour), preferred_element_type=jnp.float32)
        total = part if total is None else total + part
    return total, squares


def square_tile(square, half):
    rows = square.shape[0]
    whole = jnp.broadcast_to(jnp.sum(square, axis=1, keepdims=True), square.shape)
    high = whole.astype(jnp.bfloat16).astype(jnp.float32)
    lane = lax.broadcasted_iota(jnp.int32, square.shape, 1)
    place = lax.broadcasted_iota(jnp.int32, square.shape, 0) + rows * half
    spread = jnp.where(lane == place, high, jnp.where(lane == place + 2 * rows, whole - high, 0.0))
    return jnp.broadcast_to(jnp.sum(spread, axis=0, keepdims=True), square.shape)


def first_kernel(trivial, tab_ref, p_ref, *refs):
    v_refs, r_ref, out_refs, w_refs = refs[:2], refs[2], refs[3:5], refs[5:]
    cols, sites = p_ref.shape[2], p_ref.shape[3]
    rows = v_refs[0].shape[2]
    for colour in range(p_ref.shape[1]):
        real = p_ref[0, colour].T
        imag = p_ref[1, colour].T
        r_ref[colour, :sites, :cols] = real
        r_ref[colour, :sites, cols:] = imag
        r_ref[colour, sites:, :cols] = -imag
        r_ref[colour, sites:, cols:] = real
    total, squares = project_rows(trivial, v_refs, tab_ref, lambda colour: r_ref[colour], w_refs)
    for k, out_ref in enumerate(out_refs):
        for g in range(len(trivial)):
            at = (2 * g + k) * rows
            for part in range(2):
                out_ref[2 * g + part] = total[at : at + rows, part * cols : (part + 1) * cols]
        out_ref[2 * len(trivial)] = square_tile(squares[k], k)


def slab_kernel(v_ref, *refs):
    slab_refs, own_refs = refs[:-2], refs[-2:]
    me = lax.axis_index("tm")
    for k, ref in enumerate(slab_refs, 1):
        ref[...] = v_ref[pl.ds(2 * jnp.bitwise_xor(lax.div(me, 2), k), 2)]
    for k, ref in enumerate(own_refs):
        ref[...] = v_ref[jnp.bitwise_xor(me, k)]


def part_kernel(core_ref, *refs):
    slab_refs, out_ref = refs[:-1], refs[-1]
    for n, slab_ref in enumerate(slab_refs):
        out_ref[n] = slab_ref[1 - core_ref[0]]


def stay_kernel(trivial, core_ref, tab_ref, r_ref, *refs):
    slabs = len(refs) - 4
    slab_refs, out_ref, w_refs = refs[:slabs], refs[slabs], refs[slabs + 1 :]
    tiles, rows, cols = out_ref.shape[1:]
    v_refs = [slab_ref.at[core_ref[0]] for slab_ref in slab_refs]
    total, squares = project_rows(trivial, v_refs, tab_ref, lambda colour: r_ref[colour], w_refs)
    for n in range(slabs):
        for g in range(len(trivial)):
            low = (g * slabs + n) * rows
            for part in range(2):
                out_ref[n, 2 * g + part] = total[low : low + rows, part * cols : (part + 1) * cols]
        out_ref[n, tiles - 1] = square_tile(squares[n], 0)


def rows_kernel(trivial, where_ref, tab_ref, r_ref, own_ref, sibling_ref, stay_ref, swapped_ref, *refs):
    owners = stay_ref.shape[0] + 1
    out_refs, acc_ref, w_refs = refs[:owners], refs[owners], refs[owners + 1 :]
    tiles, rows, cols = own_ref.shape
    v_refs = [swapped_ref.at[n] for n in range(owners - 1)]
    total, squares = project_rows(trivial, v_refs, tab_ref, lambda colour: r_ref[colour], w_refs)
    last = 2 * rows * (tiles - 1)
    for tile in range(tiles - 1):
        at = 2 * rows * tile
        acc_ref[0, at : at + rows] = own_ref[tile]
        acc_ref[0, at + rows : at + 2 * rows] = sibling_ref[tile]
    acc_ref[0, last:] = own_ref[tiles - 1] + sibling_ref[tiles - 1]
    for n in range(owners - 1):
        for g in range(len(trivial)):
            low = (g * (owners - 1) + n) * rows
            for part in range(2):
                at = 2 * rows * (2 * g + part)
                acc_ref[n + 1, at : at + rows] = stay_ref[n, 2 * g + part]
                acc_ref[n + 1, at + rows : at + 2 * rows] = total[
                    low : low + rows, part * cols : (part + 1) * cols
                ]
        acc_ref[n + 1, last:] = stay_ref[n, tiles - 1] + square_tile(squares[n], 1)
    for q, out_ref in enumerate(out_refs):
        out_ref[...] = acc_ref[jnp.bitwise_xor(where_ref[0], q)].astype(out_ref.dtype)


def finish_kernel(group, core_ref, *refs):
    count = len(group)
    parts, out_ref, done_ref, sems = refs[:-3], refs[-3], refs[-2], refs[-1]
    groups = max(group) + 1
    rows = done_ref.shape[1] // 4
    last = 4 * rows * groups

    def summed(at, size):
        value = parts[0][at : at + size].astype(jnp.float32)
        for ref in parts[1:]:
            value = value + ref[at : at + size].astype(jnp.float32)
        return value

    both = jnp.broadcast_to(summed(last, rows)[:1], (2 * rows, LANES))
    lane = lax.broadcasted_iota(jnp.int32, both.shape, 1)
    place = lax.broadcasted_iota(jnp.int32, both.shape, 0)
    mine = (lane == place) | (lane == place + 2 * rows)
    squares = jnp.sum(jnp.where(mine, both, 0.0), axis=1, keepdims=True)
    inverse = lax.rsqrt(squares + epsilon_norm)
    copies = []
    for g in range(groups):
        for part in range(2):
            value = summed(2 * rows * (2 * g + part), 2 * rows) * inverse
            for other in range(2):
                first = pl.multiple_of(jnp.bitwise_xor(core_ref[0], other) * (2 * rows), 2 * rows)
                done_ref[g, pl.ds(first + part, rows, stride=2), :] = value[other * rows : (other + 1) * rows]
        for m in range(count):
            if group[m] == g:
                copies.append(pltpu.make_async_copy(done_ref.at[g], out_ref.at[m], sems.at[m]))
                copies[-1].start()
    for copy in copies:
        copy.wait()


def in_vmem(count):
    return [pl.BlockSpec(memory_space=pltpu.VMEM)] * count


def anywhere(count):
    return [pl.BlockSpec(memory_space=pl.ANY)] * count


def scalar():
    return [pl.BlockSpec(memory_space=pltpu.SMEM)]


def per_device_permutes(eigen_vectors, propagators):
    tm, space = lax.axis_size("tm"), lax.axis_size("space")
    me, z = lax.axis_index("tm"), lax.axis_index("space")
    rows, sites = eigen_vectors.shape[2], eigen_vectors.shape[4]
    cols = propagators.shape[2]
    waves, group = distinct_rows(window_waves(sites * space))
    groups = len(waves)
    trivial = tuple(not wave.any() for wave in waves)
    cosine, sine = trig_tables(waves)
    tables = np.stack([cosine, sine], 1).reshape(2 * groups, space, sites).transpose(1, 0, 2)
    table = lax.dynamic_index_in_dim(jnp.asarray(tables), z, 0, keepdims=False)

    vectors = jnp.transpose(eigen_vectors, (0, 1, 3, 2, 4))
    columns = jnp.transpose(propagators[0], (0, 2, 1, 3))
    colours = vectors.shape[2]

    def swapped(mine, r):
        return lax.ppermute(mine, "tm", [(i, i ^ r) for i in range(tm)])

    tiles = 2 * groups + 1
    tile = lambda dtype: jax.ShapeDtypeStruct((tiles, rows, cols), dtype)
    payload = lambda dtype: jax.ShapeDtypeStruct((2 * rows * (tiles - 1) + rows, cols), dtype)
    w_scratch = lambda count: [pltpu.VMEM((groups * count * rows, 2 * sites), jnp.bfloat16)] * colours
    small = pl.CostEstimate(flops=2**20, bytes_accessed=2**20, transcendentals=0)
    params = pltpu.CompilerParams(vmem_limit_bytes=12 * 2**20)

    one = lambda *lead: jax.ShapeDtypeStruct(lead + vectors.shape[1:], vectors.dtype)
    *slabs, own, sibling = pl.pallas_call(
        slab_kernel,
        out_shape=[one(2)] * (space - 1) + [one()] * 2,
        in_specs=in_vmem(1),
        out_specs=in_vmem(space + 1),
        cost_estimate=small,
        compiler_params=params,
    )(vectors)
    slabs = [swapped(slab, 2 * k) for k, slab in enumerate(slabs, 1)]
    sibling = swapped(sibling, 1)

    right, own_sums, sibling_sums = pl.pallas_call(
        functools.partial(first_kernel, trivial),
        out_shape=[jax.ShapeDtypeStruct((colours, 2 * sites, 2 * cols), jnp.bfloat16)]
        + [tile(jnp.float32)] * 2,
        in_specs=in_vmem(4),
        out_specs=in_vmem(3),
        scratch_shapes=w_scratch(2),
        cost_estimate=small,
        compiler_params=params,
    )(table, columns, own, sibling)

    where = jnp.bitwise_xor(me // 2, z).astype(jnp.int32).reshape(1)
    core = (me % 2).astype(jnp.int32).reshape(1)
    own_sums, slabs = lax.optimization_barrier((own_sums, slabs))
    part = jax.ShapeDtypeStruct((space - 1,) + slabs[0].shape[1:], slabs[0].dtype)
    leaving = pl.pallas_call(
        part_kernel,
        out_shape=part,
        in_specs=scalar() + in_vmem(len(slabs)),
        out_specs=in_vmem(1)[0],
        cost_estimate=small,
        compiler_params=params,
    )(core, *slabs)
    came = swapped(leaving, 1)
    stay_sums = pl.pallas_call(
        functools.partial(stay_kernel, trivial),
        out_shape=jax.ShapeDtypeStruct((space - 1, tiles, rows, cols), jnp.float32),
        in_specs=scalar() + in_vmem(2 + len(slabs)),
        out_specs=in_vmem(1)[0],
        scratch_shapes=w_scratch(len(slabs)),
        cost_estimate=small,
        compiler_params=params,
    )(core, table, right, *slabs)
    own, *others = pl.pallas_call(
        functools.partial(rows_kernel, trivial),
        out_shape=[payload(jnp.float32)] + [payload(jnp.bfloat16)] * (space - 1),
        in_specs=scalar() + in_vmem(6),
        out_specs=in_vmem(space),
        scratch_shapes=[pltpu.VMEM((space,) + payload(jnp.float32).shape, jnp.float32)] + w_scratch(space - 1),
        cost_estimate=small,
        compiler_params=params,
    )(where, table, right, own_sums, sibling_sums, stay_sums, came)
    parts = [own]
    for q in (2, 3, 1):
        parts.append(lax.ppermute(others[q - 1], "space", [(i, i ^ q) for i in range(space)]))
    out = pl.pallas_call(
        functools.partial(finish_kernel, group),
        out_shape=jax.ShapeDtypeStruct((len(group), 2 * rows * 2, cols), jnp.float32),
        in_specs=scalar() + in_vmem(len(parts)),
        out_specs=anywhere(1)[0],
        scratch_shapes=[
            pltpu.VMEM((groups, 2 * rows * 2, cols), jnp.float32),
            pltpu.SemaphoreType.DMA((len(group),)),
        ],
        cost_estimate=small,
        compiler_params=params,
    )(core, *parts)
    return out.reshape(len(group), 2 * rows, 1, 2, cols)


def project(vectors, columns, cosine, sine):
    slices = vectors.shape[0]
    real_in = vectors[:, 0].astype(jnp.float32)
    imag_in = vectors[:, 1].astype(jnp.float32)
    w_real = (cosine * real_in - sine * imag_in).astype(jnp.bfloat16)
    w_imag = (-(sine * real_in + cosine * imag_in)).astype(jnp.bfloat16)
    left = jnp.stack([w_real, w_imag], 1)
    left = left.reshape(slices, 2, left.shape[2], -1)
    right = columns.reshape(slices, 2, columns.shape[2], -1)
    products = jnp.einsum("tcek,tdak->etcda", left, right, preferred_element_type=jnp.float32)
    real_out = products[:, :, 0, 0] - products[:, :, 1, 1]
    imag_out = products[:, :, 0, 1] + products[:, :, 1, 0]
    return jnp.stack([real_out, imag_out], 2)


def per_device_general(eigen_vectors, propagators):
    vectors = lax.all_to_all(eigen_vectors, "tm", split_axis=0, concat_axis=2, tiled=True)
    sites = vectors.shape[4]
    space = lax.axis_size("space")
    rows = vectors.shape[2] // space
    z = lax.axis_index("space")
    squares = lax.psum(jnp.sum(jnp.square(vectors.astype(jnp.float32)), axis=(1, 3, 4)), "space")
    inverse = lax.rsqrt(squares + epsilon_norm)
    mine = lax.dynamic_slice_in_dim(inverse, z * rows, rows, 1)
    row_scale = jnp.transpose(mine)[:, :, None, None]
    waves, group = distinct_rows(window_waves(sites * space))
    positions = z * sites + jnp.arange(sites, dtype=jnp.int32)
    coords = (positions // (LS * LS), positions // LS % LS, positions % LS)
    results = []
    for g in range(len(waves)):
        momentum = momenta_table[group.index(g)]
        wave = sum(n * x for n, x in zip(momentum, coords)) % LS
        angle = wave.astype(jnp.float32) * (2.0 * math.pi / LS)
        sums = project(vectors, propagators, jnp.cos(angle), jnp.sin(angle))
        sums = lax.psum_scatter(sums, "space", scatter_dimension=0, tiled=True)
        results.append(sums * row_scale)
    return jnp.stack([results[g] for g in group], 0)


def solution(mesh):
    tm, space = mesh.shape["tm"], mesh.shape["space"]

    def per_device(eigen_vectors, propagators):
        rows, sites = eigen_vectors.shape[2], eigen_vectors.shape[4]
        fits = (
            tm == 8
            and space == 4
            and eigen_vectors.shape[0] == tm
            and rows % 16 == 0
            and sites % LANES == 0
            and propagators.shape[2] == LANES
        )
        form = per_device_permutes if fits else per_device_general
        return form(eigen_vectors, propagators)

    placed = (P(None, None, "tm", None, "space"), P("tm", None, None, None, "space"))
    return jax.shard_map(
        per_device,
        mesh=mesh,
        in_specs=placed,
        out_specs=P(None, "space", "tm", None, None),
        check_vma=False,
    )
```

```python
import functools
import math

import jax
import jax.numpy as jnp
import numpy as np
from jax import lax
from jax.experimental import pallas as pl
from jax.experimental.pallas import tpu as pltpu
from jax.sharding import PartitionSpec as P

LS = 64
LANES = 128

momenta_table = (
    (0, 0, 0),
    (1, 0, 0),
    (0, 1, 0),
    (0, 0, 1),
    (1, 1, 0),
    (1, 0, 1),
    (0, 1, 1),
    (1, 1, 1),
)
epsilon_norm = 1e-06


def window_waves(sites):
    positions = np.arange(sites)
    coords = np.stack([positions // (LS * LS), positions // LS % LS, positions % LS])
    return (np.asarray(momenta_table) @ coords) % LS


def distinct_rows(waves):
    rows, group = [], []
    for wave in waves:
        for known, row in enumerate(rows):
            if np.array_equal(row, wave):
                group.append(known)
                break
        else:
            group.append(len(rows))
            rows.append(wave)
    return np.stack(rows), tuple(group)


def trig_tables(waves):
    angle = waves.astype(np.float32) * np.float32(2.0 * math.pi / LS)
    return np.cos(angle).astype(np.float32), np.sin(angle).astype(np.float32)


def project_rows(trivial, v_refs, tab_ref, right, w_refs):
    pieces, groups = len(v_refs), len(trivial)
    colours, rows, sites = v_refs[0].shape[-3:]
    squares = [None] * pieces
    total = None
    for colour in range(colours):
        w_ref = w_refs[colour]
        for k, v_ref in enumerate(v_refs):
            real = v_ref[0, colour].astype(jnp.float32)
            imag = v_ref[1, colour].astype(jnp.float32)
            square = real * real + imag * imag
            square = sum(square[:, at : at + LANES] for at in range(0, sites, LANES))
            squares[k] = square if squares[k] is None else squares[k] + square
            for g in range(groups):
                at = (g * pieces + k) * rows
                if trivial[g]:
                    w_real, w_imag = real, -imag
                else:
                    cosine = tab_ref[2 * g : 2 * g + 1, :]
                    sine = tab_ref[2 * g + 1 : 2 * g + 2, :]
                    w_real = cosine * real - sine * imag
                    w_imag = -(sine * real + cosine * imag)
                w_ref[at : at + rows, :sites] = w_real.astype(jnp.bfloat16)
                w_ref[at : at + rows, sites:] = w_imag.astype(jnp.bfloat16)
        part = jnp.dot(w_ref[...], right(colour), preferred_element_type=jnp.float32)
        total = part if total is None else total + part
    return total, squares


def square_tile(square, half):
    rows = square.shape[0]
    whole = jnp.broadcast_to(jnp.sum(square, axis=1, keepdims=True), square.shape)
    high = whole.astype(jnp.bfloat16).astype(jnp.float32)
    lane = lax.broadcasted_iota(jnp.int32, square.shape, 1)
    place = lax.broadcasted_iota(jnp.int32, square.shape, 0) + rows * half
    spread = jnp.where(lane == place, high, jnp.where(lane == place + 2 * rows, whole - high, 0.0))
    return jnp.broadcast_to(jnp.sum(spread, axis=0, keepdims=True), square.shape)


def first_kernel(trivial, tab_ref, p_ref, *refs):
    v_refs, r_ref, out_refs, w_refs = refs[:2], refs[2], refs[3:5], refs[5:]
    cols, sites = p_ref.shape[2], p_ref.shape[3]
    rows = v_refs[0].shape[2]
    for colour in range(p_ref.shape[1]):
        real = p_ref[0, colour].T
        imag = p_ref[1, colour].T
        r_ref[colour, :sites, :cols] = real
        r_ref[colour, :sites, cols:] = imag
        r_ref[colour, sites:, :cols] = -imag
        r_ref[colour, sites:, cols:] = real
    total, squares = project_rows(trivial, v_refs, tab_ref, lambda colour: r_ref[colour], w_refs)
    for k, out_ref in enumerate(out_refs):
        for g in range(len(trivial)):
            at = (2 * g + k) * rows
            for part in range(2):
                out_ref[2 * g + part] = total[at : at + rows, part * cols : (part + 1) * cols]
        out_ref[2 * len(trivial)] = square_tile(squares[k], k)


def slab_kernel(v_ref, *refs):
    slab_refs, own_refs = refs[:-2], refs[-2:]
    me = lax.axis_index("tm")
    for k, ref in enumerate(slab_refs, 1):
        ref[...] = v_ref[pl.ds(2 * jnp.bitwise_xor(lax.div(me, 2), k), 2)]
    for k, ref in enumerate(own_refs):
        ref[...] = v_ref[jnp.bitwise_xor(me, k)]


def part_kernel(core_ref, *refs):
    slab_refs, out_ref = refs[:-1], refs[-1]
    for n, slab_ref in enumerate(slab_refs):
        out_ref[n] = slab_ref[1 - core_ref[0]]


def stay_kernel(trivial, core_ref, tab_ref, r_ref, *refs):
    slabs = len(refs) - 4
    slab_refs, out_ref, w_refs = refs[:slabs], refs[slabs], refs[slabs + 1 :]
    tiles, rows, cols = out_ref.shape[1:]
    v_refs = [slab_ref.at[core_ref[0]] for slab_ref in slab_refs]
    total, squares = project_rows(trivial, v_refs, tab_ref, lambda colour: r_ref[colour], w_refs)
    for n in range(slabs):
        for g in range(len(trivial)):
            low = (g * slabs + n) * rows
            for part in range(2):
                out_ref[n, 2 * g + part] = total[low : low + rows, part * cols : (part + 1) * cols]
        out_ref[n, tiles - 1] = square_tile(squares[n], 0)


def rows_kernel(trivial, order, where_ref, tab_ref, r_ref, own_ref, sibling_ref, stay_ref, swapped_ref, *refs):
    owners = stay_ref.shape[0] + 1
    out_refs, acc_ref, w_refs = refs[:owners], refs[owners], refs[owners + 1 :]
    tiles, rows, cols = own_ref.shape
    v_refs = [swapped_ref.at[n] for n in range(owners - 1)]
    total, squares = project_rows(trivial, v_refs, tab_ref, lambda colour: r_ref[colour], w_refs)
    last = 2 * rows * (tiles - 1)
    for tile in range(tiles - 1):
        at = 2 * rows * tile
        acc_ref[0, at : at + rows] = own_ref[tile]
        acc_ref[0, at + rows : at + 2 * rows] = sibling_ref[tile]
    acc_ref[0, last:] = own_ref[tiles - 1] + sibling_ref[tiles - 1]
    for n, k in enumerate(order):
        for g in range(len(trivial)):
            low = (g * (owners - 1) + n) * rows
            for part in range(2):
                at = 2 * rows * (2 * g + part)
                acc_ref[k, at : at + rows] = stay_ref[n, 2 * g + part]
                acc_ref[k, at + rows : at + 2 * rows] = total[
                    low : low + rows, part * cols : (part + 1) * cols
                ]
        acc_ref[k, last:] = stay_ref[n, tiles - 1] + square_tile(squares[n], 1)
    for q, out_ref in enumerate(out_refs):
        out_ref[...] = acc_ref[jnp.bitwise_xor(where_ref[0], q)].astype(out_ref.dtype)


def finish_kernel(group, core_ref, *refs):
    count = len(group)
    parts, out_ref, done_ref, sems = refs[:-3], refs[-3], refs[-2], refs[-1]
    groups = max(group) + 1
    rows = done_ref.shape[1] // 4
    last = 4 * rows * groups

    def summed(at, size):
        value = parts[0][at : at + size].astype(jnp.float32)
        for ref in parts[1:]:
            value = value + ref[at : at + size].astype(jnp.float32)
        return value

    both = jnp.broadcast_to(summed(last, rows)[:1], (2 * rows, LANES))
    lane = lax.broadcasted_iota(jnp.int32, both.shape, 1)
    place = lax.broadcasted_iota(jnp.int32, both.shape, 0)
    mine = (lane == place) | (lane == place + 2 * rows)
    squares = jnp.sum(jnp.where(mine, both, 0.0), axis=1, keepdims=True)
    inverse = lax.rsqrt(squares + epsilon_norm)
    copies = []
    for g in range(groups):
        for part in range(2):
            value = summed(2 * rows * (2 * g + part), 2 * rows) * inverse
            for other in range(2):
                first = pl.multiple_of(jnp.bitwise_xor(core_ref[0], other) * (2 * rows), 2 * rows)
                done_ref[g, pl.ds(first + part, rows, stride=2), :] = value[other * rows : (other + 1) * rows]
        for m in range(count):
            if group[m] == g:
                copies.append(pltpu.make_async_copy(done_ref.at[g], out_ref.at[m], sems.at[m]))
                copies[-1].start()
    for copy in copies:
        copy.wait()


def in_vmem(count):
    return [pl.BlockSpec(memory_space=pltpu.VMEM)] * count


def anywhere(count):
    return [pl.BlockSpec(memory_space=pl.ANY)] * count


def scalar():
    return [pl.BlockSpec(memory_space=pltpu.SMEM)]


def per_device_permutes(eigen_vectors, propagators):
    tm, space = lax.axis_size("tm"), lax.axis_size("space")
    me, z = lax.axis_index("tm"), lax.axis_index("space")
    rows, sites = eigen_vectors.shape[2], eigen_vectors.shape[4]
    cols = propagators.shape[2]
    waves, group = distinct_rows(window_waves(sites * space))
    groups = len(waves)
    trivial = tuple(not wave.any() for wave in waves)
    cosine, sine = trig_tables(waves)
    tables = np.stack([cosine, sine], 1).reshape(2 * groups, space, sites).transpose(1, 0, 2)
    table = lax.dynamic_index_in_dim(jnp.asarray(tables), z, 0, keepdims=False)

    vectors = jnp.transpose(eigen_vectors, (0, 1, 3, 2, 4))
    columns = jnp.transpose(propagators[0], (0, 2, 1, 3))
    colours = vectors.shape[2]

    def swapped(mine, r):
        return lax.ppermute(mine, "tm", [(i, i ^ r) for i in range(tm)])

    tiles = 2 * groups + 1
    tile = lambda dtype: jax.ShapeDtypeStruct((tiles, rows, cols), dtype)
    payload = lambda dtype: jax.ShapeDtypeStruct((2 * rows * (tiles - 1) + rows, cols), dtype)
    w_scratch = lambda count: [pltpu.VMEM((groups * count * rows, 2 * sites), jnp.bfloat16)] * colours
    small = pl.CostEstimate(flops=0, bytes_accessed=0, transcendentals=0)
    params = pltpu.CompilerParams(vmem_limit_bytes=12 * 2**20)

    one = lambda *lead: jax.ShapeDtypeStruct(lead + vectors.shape[1:], vectors.dtype)
    *slabs, own, sibling = pl.pallas_call(
        slab_kernel,
        out_shape=[one(2)] * (space - 1) + [one()] * 2,
        in_specs=in_vmem(1),
        out_specs=in_vmem(space + 1),
        cost_estimate=small,
        compiler_params=params,
    )(vectors)
    order = (3, 2, 1)
    slabs = [swapped(slabs[k - 1], 2 * k) for k in order]
    sibling = swapped(sibling, 1)

    right, own_sums, sibling_sums = pl.pallas_call(
        functools.partial(first_kernel, trivial),
        out_shape=[jax.ShapeDtypeStruct((colours, 2 * sites, 2 * cols), jnp.bfloat16)]
        + [tile(jnp.float32)] * 2,
        in_specs=in_vmem(4),
        out_specs=in_vmem(3),
        scratch_shapes=w_scratch(2),
        cost_estimate=small,
        compiler_params=params,
    )(table, columns, own, sibling)

    where = jnp.bitwise_xor(me // 2, z).astype(jnp.int32).reshape(1)
    core = (me % 2).astype(jnp.int32).reshape(1)
    own_sums, slabs = lax.optimization_barrier((own_sums, slabs))
    part = jax.ShapeDtypeStruct((space - 1,) + slabs[0].shape[1:], slabs[0].dtype)
    leaving = pl.pallas_call(
        part_kernel,
        out_shape=part,
        in_specs=scalar() + in_vmem(len(slabs)),
        out_specs=in_vmem(1)[0],
        cost_estimate=small,
        compiler_params=params,
    )(core, *slabs)
    came = swapped(leaving, 1)
    stay_sums = pl.pallas_call(
        functools.partial(stay_kernel, trivial),
        out_shape=jax.ShapeDtypeStruct((space - 1, tiles, rows, cols), jnp.float32),
        in_specs=scalar() + in_vmem(2 + len(slabs)),
        out_specs=in_vmem(1)[0],
        scratch_shapes=w_scratch(len(slabs)),
        cost_estimate=small,
        compiler_params=params,
    )(core, table, right, *slabs)
    own, *others = pl.pallas_call(
        functools.partial(rows_kernel, trivial, order),
        out_shape=[payload(jnp.float32)] + [payload(jnp.bfloat16)] * (space - 1),
        in_specs=scalar() + in_vmem(6),
        out_specs=in_vmem(space),
        scratch_shapes=[pltpu.VMEM((space,) + payload(jnp.float32).shape, jnp.float32)] + w_scratch(space - 1),
        cost_estimate=small,
        compiler_params=params,
    )(where, table, right, own_sums, sibling_sums, stay_sums, came)
    parts = [own]
    for q in (2, 3, 1):
        parts.append(lax.ppermute(others[q - 1], "space", [(i, i ^ q) for i in range(space)]))
    out = pl.pallas_call(
        functools.partial(finish_kernel, group),
        out_shape=jax.ShapeDtypeStruct((len(group), 2 * rows * 2, cols), jnp.float32),
        in_specs=scalar() + in_vmem(len(parts)),
        out_specs=anywhere(1)[0],
        scratch_shapes=[
            pltpu.VMEM((groups, 2 * rows * 2, cols), jnp.float32),
            pltpu.SemaphoreType.DMA((len(group),)),
        ],
        cost_estimate=small,
        compiler_params=params,
    )(core, *parts)
    return out.reshape(len(group), 2 * rows, 1, 2, cols)


def project(vectors, columns, cosine, sine):
    slices = vectors.shape[0]
    real_in = vectors[:, 0].astype(jnp.float32)
    imag_in = vectors[:, 1].astype(jnp.float32)
    w_real = (cosine * real_in - sine * imag_in).astype(jnp.bfloat16)
    w_imag = (-(sine * real_in + cosine * imag_in)).astype(jnp.bfloat16)
    left = jnp.stack([w_real, w_imag], 1)
    left = left.reshape(slices, 2, left.shape[2], -1)
    right = columns.reshape(slices, 2, columns.shape[2], -1)
    products = jnp.einsum("tcek,tdak->etcda", left, right, preferred_element_type=jnp.float32)
    real_out = products[:, :, 0, 0] - products[:, :, 1, 1]
    imag_out = products[:, :, 0, 1] + products[:, :, 1, 0]
    return jnp.stack([real_out, imag_out], 2)


def per_device_general(eigen_vectors, propagators):
    vectors = lax.all_to_all(eigen_vectors, "tm", split_axis=0, concat_axis=2, tiled=True)
    sites = vectors.shape[4]
    space = lax.axis_size("space")
    rows = vectors.shape[2] // space
    z = lax.axis_index("space")
    squares = lax.psum(jnp.sum(jnp.square(vectors.astype(jnp.float32)), axis=(1, 3, 4)), "space")
    inverse = lax.rsqrt(squares + epsilon_norm)
    mine = lax.dynamic_slice_in_dim(inverse, z * rows, rows, 1)
    row_scale = jnp.transpose(mine)[:, :, None, None]
    waves, group = distinct_rows(window_waves(sites * space))
    positions = z * sites + jnp.arange(sites, dtype=jnp.int32)
    coords = (positions // (LS * LS), positions // LS % LS, positions % LS)
    results = []
    for g in range(len(waves)):
        momentum = momenta_table[group.index(g)]
        wave = sum(n * x for n, x in zip(momentum, coords)) % LS
        angle = wave.astype(jnp.float32) * (2.0 * math.pi / LS)
        sums = project(vectors, propagators, jnp.cos(angle), jnp.sin(angle))
        sums = lax.psum_scatter(sums, "space", scatter_dimension=0, tiled=True)
        results.append(sums * row_scale)
    return jnp.stack([results[g] for g in group], 0)


def solution(mesh):
    tm, space = mesh.shape["tm"], mesh.shape["space"]

    def per_device(eigen_vectors, propagators):
        rows, sites = eigen_vectors.shape[2], eigen_vectors.shape[4]
        fits = (
            tm == 8
            and space == 4
            and eigen_vectors.shape[0] == tm
            and rows % 16 == 0
            and sites % LANES == 0
            and propagators.shape[2] == LANES
        )
        form = per_device_permutes if fits else per_device_general
        return form(eigen_vectors, propagators)

    placed = (P(None, None, "tm", None, "space"), P("tm", None, None, None, "space"))
    return jax.shard_map(
        per_device,
        mesh=mesh,
        in_specs=placed,
        out_specs=P(None, "space", "tm", None, None),
        check_vma=False,
    )
```

```python
import functools
import math

import jax
import jax.numpy as jnp
import numpy as np
from jax import lax
from jax.experimental import pallas as pl
from jax.experimental.pallas import tpu as pltpu
from jax.sharding import PartitionSpec as P

LS = 64
LANES = 128

momenta_table = (
    (0, 0, 0),
    (1, 0, 0),
    (0, 1, 0),
    (0, 0, 1),
    (1, 1, 0),
    (1, 0, 1),
    (0, 1, 1),
    (1, 1, 1),
)
epsilon_norm = 1e-06


def window_waves(sites):
    positions = np.arange(sites)
    coords = np.stack([positions // (LS * LS), positions // LS % LS, positions % LS])
    return (np.asarray(momenta_table) @ coords) % LS


def distinct_rows(waves):
    rows, group = [], []
    for wave in waves:
        for known, row in enumerate(rows):
            if np.array_equal(row, wave):
                group.append(known)
                break
        else:
            group.append(len(rows))
            rows.append(wave)
    return np.stack(rows), tuple(group)


def trig_tables(waves):
    angle = waves.astype(np.float32) * np.float32(2.0 * math.pi / LS)
    return np.cos(angle).astype(np.float32), np.sin(angle).astype(np.float32)


def project_rows(trivial, v_refs, tab_ref, right, w_refs):
    pieces, groups = len(v_refs), len(trivial)
    colours, rows, sites = v_refs[0].shape[-3:]
    squares = [None] * pieces
    total = None
    for colour in range(colours):
        w_ref = w_refs[colour]
        for k, v_ref in enumerate(v_refs):
            real = v_ref[0, colour].astype(jnp.float32)
            imag = v_ref[1, colour].astype(jnp.float32)
            square = real * real + imag * imag
            square = sum(square[:, at : at + LANES] for at in range(0, sites, LANES))
            squares[k] = square if squares[k] is None else squares[k] + square
            for g in range(groups):
                at = (g * pieces + k) * rows
                if trivial[g]:
                    w_real, w_imag = real, -imag
                else:
                    cosine = tab_ref[2 * g : 2 * g + 1, :]
                    sine = tab_ref[2 * g + 1 : 2 * g + 2, :]
                    w_real = cosine * real - sine * imag
                    w_imag = -(sine * real + cosine * imag)
                w_ref[at : at + rows, :sites] = w_real.astype(jnp.bfloat16)
                w_ref[at : at + rows, sites:] = w_imag.astype(jnp.bfloat16)
        part = jnp.dot(w_ref[...], right(colour), preferred_element_type=jnp.float32)
        total = part if total is None else total + part
    return total, squares


def square_tile(square, half):
    rows = square.shape[0]
    whole = jnp.broadcast_to(jnp.sum(square, axis=1, keepdims=True), square.shape)
    high = whole.astype(jnp.bfloat16).astype(jnp.float32)
    lane = lax.broadcasted_iota(jnp.int32, square.shape, 1)
    place = lax.broadcasted_iota(jnp.int32, square.shape, 0) + rows * half
    spread = jnp.where(lane == place, high, jnp.where(lane == place + 2 * rows, whole - high, 0.0))
    return jnp.broadcast_to(jnp.sum(spread, axis=0, keepdims=True), square.shape)


def first_kernel(trivial, tab_ref, p_ref, *refs):
    v_refs, r_ref, out_refs, w_refs = refs[:2], refs[2], refs[3:5], refs[5:]
    cols, sites = p_ref.shape[2], p_ref.shape[3]
    rows = v_refs[0].shape[2]
    for colour in range(p_ref.shape[1]):
        real = p_ref[0, colour].T
        imag = p_ref[1, colour].T
        r_ref[colour, :sites, :cols] = real
        r_ref[colour, :sites, cols:] = imag
        r_ref[colour, sites:, :cols] = -imag
        r_ref[colour, sites:, cols:] = real
    total, squares = project_rows(trivial, v_refs, tab_ref, lambda colour: r_ref[colour], w_refs)
    for k, out_ref in enumerate(out_refs):
        for g in range(len(trivial)):
            at = (2 * g + k) * rows
            for part in range(2):
                out_ref[2 * g + part] = total[at : at + rows, part * cols : (part + 1) * cols]
        out_ref[2 * len(trivial)] = square_tile(squares[k], k)


def slab_kernel(v_ref, *refs):
    slab_refs, own_refs = refs[:-2], refs[-2:]
    me = lax.axis_index("tm")
    for k, ref in enumerate(slab_refs, 1):
        ref[...] = v_ref[pl.ds(2 * jnp.bitwise_xor(lax.div(me, 2), k), 2)]
    for k, ref in enumerate(own_refs):
        ref[...] = v_ref[jnp.bitwise_xor(me, k)]


def part_kernel(core_ref, *refs):
    slab_refs, out_ref = refs[:-1], refs[-1]
    for n, slab_ref in enumerate(slab_refs):
        out_ref[n] = slab_ref[1 - core_ref[0]]


def sums_kernel(trivial, half, core_ref, tab_ref, r_ref, *refs):
    given = len(refs) - 1 - r_ref.shape[0]
    out_ref, w_refs = refs[given], refs[given + 1 :]
    count, tiles, rows, cols = out_ref.shape
    if half == 0:
        v_refs = [slab_ref.at[core_ref[0]] for slab_ref in refs[:given]]
    else:
        v_refs = [refs[0].at[n] for n in range(count)]
    total, squares = project_rows(trivial, v_refs, tab_ref, lambda colour: r_ref[colour], w_refs)
    for n in range(count):
        for g in range(len(trivial)):
            low = (g * count + n) * rows
            for part in range(2):
                out_ref[n, 2 * g + part] = total[low : low + rows, part * cols : (part + 1) * cols]
        out_ref[n, tiles - 1] = square_tile(squares[n], half)


def rows_kernel(trivial, order, where_ref, tab_ref, r_ref, *refs):
    own_ref, sibling_ref, stay_ref, came_ref, last_stay_ref, last_v_ref = refs[:6]
    owners = len(order) + 1
    early = stay_ref.shape[0]
    late = owners - 1 - early
    out_refs, acc_ref, w_refs = refs[6 : 6 + owners], refs[6 + owners], refs[7 + owners :]
    tiles, rows, cols = own_ref.shape
    v_refs = [last_v_ref.at[n] for n in range(late)]
    total, squares = project_rows(trivial, v_refs, tab_ref, lambda colour: r_ref[colour], w_refs)
    halves = [(0, [own_ref[n] for n in range(tiles)], [sibling_ref[n] for n in range(tiles)])]
    for n, k in enumerate(order[:early]):
        halves.append((k, [stay_ref[n, i] for i in range(tiles)], [came_ref[n, i] for i in range(tiles)]))
    for n, k in enumerate(order[early:]):
        right = [
            total[(g * late + n) * rows : (g * late + n + 1) * rows, part * cols : (part + 1) * cols]
            for g in range(len(trivial))
            for part in range(2)
        ]
        right.append(square_tile(squares[n], 1))
        halves.append((k, [last_stay_ref[n, i] for i in range(tiles)], right))
    for k, left, right in halves:
        for tile in range(tiles - 1):
            at = 2 * rows * tile
            acc_ref[k, at : at + rows] = left[tile]
            acc_ref[k, at + rows : at + 2 * rows] = right[tile]
        acc_ref[k, 2 * rows * (tiles - 1) :] = left[tiles - 1] + right[tiles - 1]
    for q, out_ref in enumerate(out_refs):
        out_ref[...] = acc_ref[jnp.bitwise_xor(where_ref[0], q)].astype(out_ref.dtype)


def finish_kernel(group, core_ref, *refs):
    count = len(group)
    parts, out_ref, done_ref, sems = refs[:-3], refs[-3], refs[-2], refs[-1]
    groups = max(group) + 1
    rows = done_ref.shape[1] // 4
    last = 4 * rows * groups

    def summed(at, size):
        value = parts[0][at : at + size].astype(jnp.float32)
        for ref in parts[1:]:
            value = value + ref[at : at + size].astype(jnp.float32)
        return value

    both = jnp.broadcast_to(summed(last, rows)[:1], (2 * rows, LANES))
    lane = lax.broadcasted_iota(jnp.int32, both.shape, 1)
    place = lax.broadcasted_iota(jnp.int32, both.shape, 0)
    mine = (lane == place) | (lane == place + 2 * rows)
    squares = jnp.sum(jnp.where(mine, both, 0.0), axis=1, keepdims=True)
    inverse = lax.rsqrt(squares + epsilon_norm)
    copies = []
    for g in range(groups):
        for part in range(2):
            value = summed(2 * rows * (2 * g + part), 2 * rows) * inverse
            for other in range(2):
                first = pl.multiple_of(jnp.bitwise_xor(core_ref[0], other) * (2 * rows), 2 * rows)
                done_ref[g, pl.ds(first + part, rows, stride=2), :] = value[other * rows : (other + 1) * rows]
        for m in range(count):
            if group[m] == g:
                copies.append(pltpu.make_async_copy(done_ref.at[g], out_ref.at[m], sems.at[m]))
                copies[-1].start()
    for copy in copies:
        copy.wait()


def in_vmem(count):
    return [pl.BlockSpec(memory_space=pltpu.VMEM)] * count


def anywhere(count):
    return [pl.BlockSpec(memory_space=pl.ANY)] * count


def scalar():
    return [pl.BlockSpec(memory_space=pltpu.SMEM)]


def per_device_permutes(eigen_vectors, propagators):
    tm, space = lax.axis_size("tm"), lax.axis_size("space")
    me, z = lax.axis_index("tm"), lax.axis_index("space")
    rows, sites = eigen_vectors.shape[2], eigen_vectors.shape[4]
    cols = propagators.shape[2]
    waves, group = distinct_rows(window_waves(sites * space))
    groups = len(waves)
    trivial = tuple(not wave.any() for wave in waves)
    cosine, sine = trig_tables(waves)
    tables = np.stack([cosine, sine], 1).reshape(2 * groups, space, sites).transpose(1, 0, 2)
    table = lax.dynamic_index_in_dim(jnp.asarray(tables), z, 0, keepdims=False)

    vectors = jnp.transpose(eigen_vectors, (0, 1, 3, 2, 4))
    columns = jnp.transpose(propagators[0], (0, 2, 1, 3))
    colours = vectors.shape[2]

    def swapped(mine, r):
        return lax.ppermute(mine, "tm", [(i, i ^ r) for i in range(tm)])

    tiles = 2 * groups + 1
    tile = lambda dtype: jax.ShapeDtypeStruct((tiles, rows, cols), dtype)
    payload = lambda dtype: jax.ShapeDtypeStruct((2 * rows * (tiles - 1) + rows, cols), dtype)
    w_scratch = lambda count: [pltpu.VMEM((groups * count * rows, 2 * sites), jnp.bfloat16)] * colours
    small = pl.CostEstimate(flops=0, bytes_accessed=0, transcendentals=0)
    params = pltpu.CompilerParams(vmem_limit_bytes=12 * 2**20)

    one = lambda *lead: jax.ShapeDtypeStruct(lead + vectors.shape[1:], vectors.dtype)
    *slabs, own, sibling = pl.pallas_call(
        slab_kernel,
        out_shape=[one(2)] * (space - 1) + [one()] * 2,
        in_specs=in_vmem(1),
        out_specs=in_vmem(space + 1),
        cost_estimate=small,
        compiler_params=params,
    )(vectors)
    order, cut = (2, 1, 3), 2
    slabs = [swapped(slabs[k - 1], 2 * k) for k in order]
    sibling = swapped(sibling, 1)

    right, own_sums, sibling_sums = pl.pallas_call(
        functools.partial(first_kernel, trivial),
        out_shape=[jax.ShapeDtypeStruct((colours, 2 * sites, 2 * cols), jnp.bfloat16)]
        + [tile(jnp.float32)] * 2,
        in_specs=in_vmem(4),
        out_specs=in_vmem(3),
        scratch_shapes=w_scratch(2),
        cost_estimate=small,
        compiler_params=params,
    )(table, columns, own, sibling)

    where = jnp.bitwise_xor(me // 2, z).astype(jnp.int32).reshape(1)
    core = (me % 2).astype(jnp.int32).reshape(1)
    def part_of(slabs):
        leaving = pl.pallas_call(
            part_kernel,
            out_shape=one(len(slabs)),
            in_specs=scalar() + in_vmem(len(slabs)),
            out_specs=in_vmem(1)[0],
            cost_estimate=small,
            compiler_params=params,
        )(core, *slabs)
        return swapped(leaving, 1)

    def sums_of(half, count, *pieces):
        return pl.pallas_call(
            functools.partial(sums_kernel, trivial, half),
            out_shape=jax.ShapeDtypeStruct((count, tiles, rows, cols), jnp.float32),
            in_specs=scalar() + in_vmem(2 + len(pieces)),
            out_specs=in_vmem(1)[0],
            scratch_shapes=w_scratch(count),
            cost_estimate=small,
            compiler_params=params,
        )(core, table, right, *pieces)

    own_sums, early = lax.optimization_barrier((own_sums, slabs[:cut]))
    stay_sums = sums_of(0, len(early), *early)
    came_sums = sums_of(1, len(early), part_of(early))
    stay_sums, late = lax.optimization_barrier((stay_sums, slabs[cut:]))
    last_sums = sums_of(0, len(late), *late)
    own, *others = pl.pallas_call(
        functools.partial(rows_kernel, trivial, order),
        out_shape=[payload(jnp.float32)] + [payload(jnp.bfloat16)] * (space - 1),
        in_specs=scalar() + in_vmem(8),
        out_specs=in_vmem(space),
        scratch_shapes=[pltpu.VMEM((space,) + payload(jnp.float32).shape, jnp.float32)] + w_scratch(len(late)),
        cost_estimate=small,
        compiler_params=params,
    )(where, table, right, own_sums, sibling_sums, stay_sums, came_sums, last_sums, part_of(late))
    parts = [own]
    for q in (2, 3, 1):
        parts.append(lax.ppermute(others[q - 1], "space", [(i, i ^ q) for i in range(space)]))
    out = pl.pallas_call(
        functools.partial(finish_kernel, group),
        out_shape=jax.ShapeDtypeStruct((len(group), 2 * rows * 2, cols), jnp.float32),
        in_specs=scalar() + in_vmem(len(parts)),
        out_specs=anywhere(1)[0],
        scratch_shapes=[
            pltpu.VMEM((groups, 2 * rows * 2, cols), jnp.float32),
            pltpu.SemaphoreType.DMA((len(group),)),
        ],
        cost_estimate=small,
        compiler_params=params,
    )(core, *parts)
    return out.reshape(len(group), 2 * rows, 1, 2, cols)


def project(vectors, columns, cosine, sine):
    slices = vectors.shape[0]
    real_in = vectors[:, 0].astype(jnp.float32)
    imag_in = vectors[:, 1].astype(jnp.float32)
    w_real = (cosine * real_in - sine * imag_in).astype(jnp.bfloat16)
    w_imag = (-(sine * real_in + cosine * imag_in)).astype(jnp.bfloat16)
    left = jnp.stack([w_real, w_imag], 1)
    left = left.reshape(slices, 2, left.shape[2], -1)
    right = columns.reshape(slices, 2, columns.shape[2], -1)
    products = jnp.einsum("tcek,tdak->etcda", left, right, preferred_element_type=jnp.float32)
    real_out = products[:, :, 0, 0] - products[:, :, 1, 1]
    imag_out = products[:, :, 0, 1] + products[:, :, 1, 0]
    return jnp.stack([real_out, imag_out], 2)


def per_device_general(eigen_vectors, propagators):
    vectors = lax.all_to_all(eigen_vectors, "tm", split_axis=0, concat_axis=2, tiled=True)
    sites = vectors.shape[4]
    space = lax.axis_size("space")
    rows = vectors.shape[2] // space
    z = lax.axis_index("space")
    squares = lax.psum(jnp.sum(jnp.square(vectors.astype(jnp.float32)), axis=(1, 3, 4)), "space")
    inverse = lax.rsqrt(squares + epsilon_norm)
    mine = lax.dynamic_slice_in_dim(inverse, z * rows, rows, 1)
    row_scale = jnp.transpose(mine)[:, :, None, None]
    waves, group = distinct_rows(window_waves(sites * space))
    positions = z * sites + jnp.arange(sites, dtype=jnp.int32)
    coords = (positions // (LS * LS), positions // LS % LS, positions % LS)
    results = []
    for g in range(len(waves)):
        momentum = momenta_table[group.index(g)]
        wave = sum(n * x for n, x in zip(momentum, coords)) % LS
        angle = wave.astype(jnp.float32) * (2.0 * math.pi / LS)
        sums = project(vectors, propagators, jnp.cos(angle), jnp.sin(angle))
        sums = lax.psum_scatter(sums, "space", scatter_dimension=0, tiled=True)
        results.append(sums * row_scale)
    return jnp.stack([results[g] for g in group], 0)


def solution(mesh):
    tm, space = mesh.shape["tm"], mesh.shape["space"]

    def per_device(eigen_vectors, propagators):
        rows, sites = eigen_vectors.shape[2], eigen_vectors.shape[4]
        fits = (
            tm == 8
            and space == 4
            and eigen_vectors.shape[0] == tm
            and rows % 16 == 0
            and sites % LANES == 0
            and propagators.shape[2] == LANES
        )
        form = per_device_permutes if fits else per_device_general
        return form(eigen_vectors, propagators)

    placed = (P(None, None, "tm", None, "space"), P("tm", None, None, None, "space"))
    return jax.shard_map(
        per_device,
        mesh=mesh,
        in_specs=placed,
        out_specs=P(None, "space", "tm", None, None),
        check_vma=False,
    )
```

```python
import functools
import math

import jax
import jax.numpy as jnp
import numpy as np
from jax import lax
from jax.experimental import pallas as pl
from jax.experimental.pallas import tpu as pltpu
from jax.sharding import PartitionSpec as P

LS = 64
LANES = 128

momenta_table = (
    (0, 0, 0),
    (1, 0, 0),
    (0, 1, 0),
    (0, 0, 1),
    (1, 1, 0),
    (1, 0, 1),
    (0, 1, 1),
    (1, 1, 1),
)
epsilon_norm = 1e-06


def window_waves(sites):
    positions = np.arange(sites)
    coords = np.stack([positions // (LS * LS), positions // LS % LS, positions % LS])
    return (np.asarray(momenta_table) @ coords) % LS


def distinct_rows(waves):
    rows, group = [], []
    for wave in waves:
        for known, row in enumerate(rows):
            if np.array_equal(row, wave):
                group.append(known)
                break
        else:
            group.append(len(rows))
            rows.append(wave)
    return np.stack(rows), tuple(group)


def trig_tables(waves):
    angle = waves.astype(np.float32) * np.float32(2.0 * math.pi / LS)
    return np.cos(angle).astype(np.float32), np.sin(angle).astype(np.float32)


def project_rows(trivial, v_refs, tab_ref, right, w_refs):
    pieces, groups = len(v_refs), len(trivial)
    colours, rows, sites = v_refs[0].shape[-3:]
    squares = [None] * pieces
    total = None
    for colour in range(colours):
        w_ref = w_refs[colour]
        for k, v_ref in enumerate(v_refs):
            real = v_ref[0, colour].astype(jnp.float32)
            imag = v_ref[1, colour].astype(jnp.float32)
            square = real * real + imag * imag
            square = sum(square[:, at : at + LANES] for at in range(0, sites, LANES))
            squares[k] = square if squares[k] is None else squares[k] + square
            for g in range(groups):
                at = (g * pieces + k) * rows
                if trivial[g]:
                    w_real, w_imag = real, -imag
                else:
                    cosine = tab_ref[2 * g : 2 * g + 1, :]
                    sine = tab_ref[2 * g + 1 : 2 * g + 2, :]
                    w_real = cosine * real - sine * imag
                    w_imag = -(sine * real + cosine * imag)
                w_ref[at : at + rows, :sites] = w_real.astype(jnp.bfloat16)
                w_ref[at : at + rows, sites:] = w_imag.astype(jnp.bfloat16)
        part = jnp.dot(w_ref[...], right(colour), preferred_element_type=jnp.float32)
        total = part if total is None else total + part
    return total, squares


def square_tile(square, half):
    rows = square.shape[0]
    whole = jnp.broadcast_to(jnp.sum(square, axis=1, keepdims=True), square.shape)
    high = whole.astype(jnp.bfloat16).astype(jnp.float32)
    lane = lax.broadcasted_iota(jnp.int32, square.shape, 1)
    place = lax.broadcasted_iota(jnp.int32, square.shape, 0) + rows * half
    spread = jnp.where(lane == place, high, jnp.where(lane == place + 2 * rows, whole - high, 0.0))
    return jnp.broadcast_to(jnp.sum(spread, axis=0, keepdims=True), square.shape)


def first_kernel(trivial, tab_ref, p_ref, *refs):
    v_refs, r_ref, out_refs, w_refs = refs[:2], refs[2], refs[3:5], refs[5:]
    cols, sites = p_ref.shape[2], p_ref.shape[3]
    rows = v_refs[0].shape[2]
    for colour in range(p_ref.shape[1]):
        real = p_ref[0, colour].T
        imag = p_ref[1, colour].T
        r_ref[colour, :sites, :cols] = real
        r_ref[colour, :sites, cols:] = imag
        r_ref[colour, sites:, :cols] = -imag
        r_ref[colour, sites:, cols:] = real
    total, squares = project_rows(trivial, v_refs, tab_ref, lambda colour: r_ref[colour], w_refs)
    for k, out_ref in enumerate(out_refs):
        for g in range(len(trivial)):
            at = (2 * g + k) * rows
            for part in range(2):
                out_ref[2 * g + part] = total[at : at + rows, part * cols : (part + 1) * cols]
        out_ref[2 * len(trivial)] = square_tile(squares[k], k)


def slab_kernel(v_ref, *refs):
    slab_refs, own_refs = refs[:-2], refs[-2:]
    me = lax.axis_index("tm")
    for k, ref in enumerate(slab_refs, 1):
        ref[...] = v_ref[pl.ds(2 * jnp.bitwise_xor(lax.div(me, 2), k), 2)]
    for k, ref in enumerate(own_refs):
        ref[...] = v_ref[jnp.bitwise_xor(me, k)]


def part_kernel(core_ref, *refs):
    slab_refs, out_ref = refs[:-1], refs[-1]
    for n, slab_ref in enumerate(slab_refs):
        out_ref[n] = slab_ref[1 - core_ref[0]]


def sums_kernel(trivial, half, core_ref, tab_ref, r_ref, *refs):
    given = len(refs) - 1 - r_ref.shape[0]
    out_ref, w_refs = refs[given], refs[given + 1 :]
    count, tiles, rows, cols = out_ref.shape
    if half == 0:
        v_refs = [slab_ref.at[core_ref[0]] for slab_ref in refs[:given]]
    else:
        v_refs = [refs[0].at[n] for n in range(count)]
    total, squares = project_rows(trivial, v_refs, tab_ref, lambda colour: r_ref[colour], w_refs)
    for n in range(count):
        for g in range(len(trivial)):
            low = (g * count + n) * rows
            for part in range(2):
                out_ref[n, 2 * g + part] = total[low : low + rows, part * cols : (part + 1) * cols]
        out_ref[n, tiles - 1] = square_tile(squares[n], half)


def rows_kernel(trivial, order, where_ref, tab_ref, r_ref, *refs):
    own_ref, sibling_ref, stay_ref, came_ref, last_stay_ref, last_v_ref = refs[:6]
    owners = len(order) + 1
    early = stay_ref.shape[0]
    late = owners - 1 - early
    out_refs, acc_ref, w_refs = refs[6 : 6 + owners], refs[6 + owners], refs[7 + owners :]
    tiles, rows, cols = own_ref.shape
    v_refs = [last_v_ref.at[n] for n in range(late)]
    total, squares = project_rows(trivial, v_refs, tab_ref, lambda colour: r_ref[colour], w_refs)
    halves = [(0, [own_ref[n] for n in range(tiles)], [sibling_ref[n] for n in range(tiles)])]
    for n, k in enumerate(order[:early]):
        halves.append((k, [stay_ref[n, i] for i in range(tiles)], [came_ref[n, i] for i in range(tiles)]))
    for n, k in enumerate(order[early:]):
        right = [
            total[(g * late + n) * rows : (g * late + n + 1) * rows, part * cols : (part + 1) * cols]
            for g in range(len(trivial))
            for part in range(2)
        ]
        right.append(square_tile(squares[n], 1))
        halves.append((k, [last_stay_ref[n, i] for i in range(tiles)], right))
    for k, left, right in halves:
        for tile in range(tiles - 1):
            at = 2 * rows * tile
            acc_ref[k, at : at + rows] = left[tile]
            acc_ref[k, at + rows : at + 2 * rows] = right[tile]
        acc_ref[k, 2 * rows * (tiles - 1) :] = left[tiles - 1] + right[tiles - 1]
    for q, out_ref in enumerate(out_refs):
        out_ref[...] = acc_ref[jnp.bitwise_xor(where_ref[0], q)].astype(out_ref.dtype)


def finish_kernel(group, core_ref, *refs):
    count = len(group)
    parts, out_ref = refs[:-1], refs[-1]
    groups = max(group) + 1
    rows = out_ref.shape[1] // 4
    last = 4 * rows * groups

    def summed(at, size):
        value = parts[0][at : at + size].astype(jnp.float32)
        for ref in parts[1:]:
            value = value + ref[at : at + size].astype(jnp.float32)
        return value

    both = jnp.broadcast_to(summed(last, rows)[:1], (2 * rows, LANES))
    lane = lax.broadcasted_iota(jnp.int32, both.shape, 1)
    place = lax.broadcasted_iota(jnp.int32, both.shape, 0)
    mine = (lane == place) | (lane == place + 2 * rows)
    squares = jnp.sum(jnp.where(mine, both, 0.0), axis=1, keepdims=True)
    inverse = lax.rsqrt(squares + epsilon_norm)
    for g in range(groups):
        for part in range(2):
            value = summed(2 * rows * (2 * g + part), 2 * rows) * inverse
            for other in range(2):
                first = pl.multiple_of(jnp.bitwise_xor(core_ref[0], other) * (2 * rows), 2 * rows)
                half = value[other * rows : (other + 1) * rows]
                for m in range(count):
                    if group[m] == g:
                        out_ref[m, pl.ds(first + part, rows, stride=2), :] = half


def in_vmem(count):
    return [pl.BlockSpec(memory_space=pltpu.VMEM)] * count


def scalar():
    return [pl.BlockSpec(memory_space=pltpu.SMEM)]


def per_device_permutes(eigen_vectors, propagators):
    tm, space = lax.axis_size("tm"), lax.axis_size("space")
    me, z = lax.axis_index("tm"), lax.axis_index("space")
    rows, sites = eigen_vectors.shape[2], eigen_vectors.shape[4]
    cols = propagators.shape[2]
    waves, group = distinct_rows(window_waves(sites * space))
    groups = len(waves)
    trivial = tuple(not wave.any() for wave in waves)
    cosine, sine = trig_tables(waves)
    tables = np.stack([cosine, sine], 1).reshape(2 * groups, space, sites).transpose(1, 0, 2)
    table = lax.dynamic_index_in_dim(jnp.asarray(tables), z, 0, keepdims=False)

    vectors = jnp.transpose(eigen_vectors, (0, 1, 3, 2, 4))
    columns = jnp.transpose(propagators[0], (0, 2, 1, 3))
    colours = vectors.shape[2]

    def swapped(mine, r):
        return lax.ppermute(mine, "tm", [(i, i ^ r) for i in range(tm)])

    tiles = 2 * groups + 1
    tile = lambda dtype: jax.ShapeDtypeStruct((tiles, rows, cols), dtype)
    payload = lambda dtype: jax.ShapeDtypeStruct((2 * rows * (tiles - 1) + rows, cols), dtype)
    w_scratch = lambda count: [pltpu.VMEM((groups * count * rows, 2 * sites), jnp.bfloat16)] * colours
    small = pl.CostEstimate(flops=0, bytes_accessed=0, transcendentals=0)
    params = pltpu.CompilerParams(vmem_limit_bytes=12 * 2**20)

    one = lambda *lead: jax.ShapeDtypeStruct(lead + vectors.shape[1:], vectors.dtype)
    *slabs, own, sibling = pl.pallas_call(
        slab_kernel,
        out_shape=[one(2)] * (space - 1) + [one()] * 2,
        in_specs=in_vmem(1),
        out_specs=in_vmem(space + 1),
        cost_estimate=small,
        compiler_params=params,
    )(vectors)
    order, cut = (2, 1, 3), 2
    slabs = [swapped(slabs[k - 1], 2 * k) for k in order]
    sibling = swapped(sibling, 1)

    right, own_sums, sibling_sums = pl.pallas_call(
        functools.partial(first_kernel, trivial),
        out_shape=[jax.ShapeDtypeStruct((colours, 2 * sites, 2 * cols), jnp.bfloat16)]
        + [tile(jnp.float32)] * 2,
        in_specs=in_vmem(4),
        out_specs=in_vmem(3),
        scratch_shapes=w_scratch(2),
        cost_estimate=small,
        compiler_params=params,
    )(table, columns, own, sibling)

    where = jnp.bitwise_xor(me // 2, z).astype(jnp.int32).reshape(1)
    core = (me % 2).astype(jnp.int32).reshape(1)
    def part_of(slabs):
        leaving = pl.pallas_call(
            part_kernel,
            out_shape=one(len(slabs)),
            in_specs=scalar() + in_vmem(len(slabs)),
            out_specs=in_vmem(1)[0],
            cost_estimate=small,
            compiler_params=params,
        )(core, *slabs)
        return swapped(leaving, 1)

    def sums_of(half, count, *pieces):
        return pl.pallas_call(
            functools.partial(sums_kernel, trivial, half),
            out_shape=jax.ShapeDtypeStruct((count, tiles, rows, cols), jnp.float32),
            in_specs=scalar() + in_vmem(2 + len(pieces)),
            out_specs=in_vmem(1)[0],
            scratch_shapes=w_scratch(count),
            cost_estimate=small,
            compiler_params=params,
        )(core, table, right, *pieces)

    own_sums, early = lax.optimization_barrier((own_sums, slabs[:cut]))
    stay_sums = sums_of(0, len(early), *early)
    came_sums = sums_of(1, len(early), part_of(early))
    stay_sums, late = lax.optimization_barrier((stay_sums, slabs[cut:]))
    last_sums = sums_of(0, len(late), *late)
    own, *others = pl.pallas_call(
        functools.partial(rows_kernel, trivial, order),
        out_shape=[payload(jnp.float32)] + [payload(jnp.bfloat16)] * (space - 1),
        in_specs=scalar() + in_vmem(8),
        out_specs=in_vmem(space),
        scratch_shapes=[pltpu.VMEM((space,) + payload(jnp.float32).shape, jnp.float32)] + w_scratch(len(late)),
        cost_estimate=small,
        compiler_params=params,
    )(where, table, right, own_sums, sibling_sums, stay_sums, came_sums, last_sums, part_of(late))
    parts = [own]
    for q in (2, 3, 1):
        parts.append(lax.ppermute(others[q - 1], "space", [(i, i ^ q) for i in range(space)]))
    out = pl.pallas_call(
        functools.partial(finish_kernel, group),
        out_shape=jax.ShapeDtypeStruct((len(group), 2 * rows * 2, cols), jnp.float32),
        in_specs=scalar() + in_vmem(len(parts)),
        out_specs=in_vmem(1)[0],
        cost_estimate=small,
        compiler_params=params,
    )(core, *parts)
    return out.reshape(len(group), 2 * rows, 1, 2, cols)


def project(vectors, columns, cosine, sine):
    slices = vectors.shape[0]
    real_in = vectors[:, 0].astype(jnp.float32)
    imag_in = vectors[:, 1].astype(jnp.float32)
    w_real = (cosine * real_in - sine * imag_in).astype(jnp.bfloat16)
    w_imag = (-(sine * real_in + cosine * imag_in)).astype(jnp.bfloat16)
    left = jnp.stack([w_real, w_imag], 1)
    left = left.reshape(slices, 2, left.shape[2], -1)
    right = columns.reshape(slices, 2, columns.shape[2], -1)
    products = jnp.einsum("tcek,tdak->etcda", left, right, preferred_element_type=jnp.float32)
    real_out = products[:, :, 0, 0] - products[:, :, 1, 1]
    imag_out = products[:, :, 0, 1] + products[:, :, 1, 0]
    return jnp.stack([real_out, imag_out], 2)


def per_device_general(eigen_vectors, propagators):
    vectors = lax.all_to_all(eigen_vectors, "tm", split_axis=0, concat_axis=2, tiled=True)
    sites = vectors.shape[4]
    space = lax.axis_size("space")
    rows = vectors.shape[2] // space
    z = lax.axis_index("space")
    squares = lax.psum(jnp.sum(jnp.square(vectors.astype(jnp.float32)), axis=(1, 3, 4)), "space")
    inverse = lax.rsqrt(squares + epsilon_norm)
    mine = lax.dynamic_slice_in_dim(inverse, z * rows, rows, 1)
    row_scale = jnp.transpose(mine)[:, :, None, None]
    waves, group = distinct_rows(window_waves(sites * space))
    positions = z * sites + jnp.arange(sites, dtype=jnp.int32)
    coords = (positions // (LS * LS), positions // LS % LS, positions % LS)
    results = []
    for g in range(len(waves)):
        momentum = momenta_table[group.index(g)]
        wave = sum(n * x for n, x in zip(momentum, coords)) % LS
        angle = wave.astype(jnp.float32) * (2.0 * math.pi / LS)
        sums = project(vectors, propagators, jnp.cos(angle), jnp.sin(angle))
        sums = lax.psum_scatter(sums, "space", scatter_dimension=0, tiled=True)
        results.append(sums * row_scale)
    return jnp.stack([results[g] for g in group], 0)


def solution(mesh):
    tm, space = mesh.shape["tm"], mesh.shape["space"]

    def per_device(eigen_vectors, propagators):
        rows, sites = eigen_vectors.shape[2], eigen_vectors.shape[4]
        fits = (
            tm == 8
            and space == 4
            and eigen_vectors.shape[0] == tm
            and rows % 16 == 0
            and sites % LANES == 0
            and propagators.shape[2] == LANES
        )
        form = per_device_permutes if fits else per_device_general
        return form(eigen_vectors, propagators)

    placed = (P(None, None, "tm", None, "space"), P("tm", None, None, None, "space"))
    return jax.shard_map(
        per_device,
        mesh=mesh,
        in_specs=placed,
        out_specs=P(None, "space", "tm", None, None),
        check_vma=False,
    )
```

```python
import functools
import math

import jax
import jax.numpy as jnp
import numpy as np
from jax import lax
from jax.experimental import pallas as pl
from jax.experimental.pallas import tpu as pltpu
from jax.sharding import PartitionSpec as P

LS = 64
LANES = 128

momenta_table = (
    (0, 0, 0),
    (1, 0, 0),
    (0, 1, 0),
    (0, 0, 1),
    (1, 1, 0),
    (1, 0, 1),
    (0, 1, 1),
    (1, 1, 1),
)
epsilon_norm = 1e-06


def window_waves(sites):
    positions = np.arange(sites)
    coords = np.stack([positions // (LS * LS), positions // LS % LS, positions % LS])
    return (np.asarray(momenta_table) @ coords) % LS


def distinct_rows(waves):
    rows, group = [], []
    for wave in waves:
        for known, row in enumerate(rows):
            if np.array_equal(row, wave):
                group.append(known)
                break
        else:
            group.append(len(rows))
            rows.append(wave)
    return np.stack(rows), tuple(group)


def trig_tables(waves):
    angle = waves.astype(np.float32) * np.float32(2.0 * math.pi / LS)
    return np.cos(angle).astype(np.float32), np.sin(angle).astype(np.float32)


def project_rows(trivial, v_refs, tab_ref, right, w_refs):
    pieces, groups = len(v_refs), len(trivial)
    colours, rows, sites = v_refs[0].shape[-3:]
    squares = [None] * pieces
    total = None
    for colour in range(colours):
        w_ref = w_refs[colour]
        for k, v_ref in enumerate(v_refs):
            real = v_ref[0, colour].astype(jnp.float32)
            imag = v_ref[1, colour].astype(jnp.float32)
            square = real * real + imag * imag
            square = sum(square[:, at : at + LANES] for at in range(0, sites, LANES))
            squares[k] = square if squares[k] is None else squares[k] + square
            for g in range(groups):
                at = (g * pieces + k) * rows
                if trivial[g]:
                    w_real, w_imag = real, -imag
                else:
                    cosine = tab_ref[2 * g : 2 * g + 1, :]
                    sine = tab_ref[2 * g + 1 : 2 * g + 2, :]
                    w_real = cosine * real - sine * imag
                    w_imag = -(sine * real + cosine * imag)
                w_ref[at : at + rows, :sites] = w_real.astype(jnp.bfloat16)
                w_ref[at : at + rows, sites:] = w_imag.astype(jnp.bfloat16)
        part = jnp.dot(w_ref[...], right(colour), preferred_element_type=jnp.float32)
        total = part if total is None else total + part
    return total, squares


def square_tile(square, half):
    rows = square.shape[0]
    whole = jnp.broadcast_to(jnp.sum(square, axis=1, keepdims=True), square.shape)
    high = whole.astype(jnp.bfloat16).astype(jnp.float32)
    lane = lax.broadcasted_iota(jnp.int32, square.shape, 1)
    place = lax.broadcasted_iota(jnp.int32, square.shape, 0) + rows * half
    spread = jnp.where(lane == place, high, jnp.where(lane == place + 2 * rows, whole - high, 0.0))
    return jnp.broadcast_to(jnp.sum(spread, axis=0, keepdims=True), square.shape)


def first_kernel(trivial, tab_ref, p_ref, *refs):
    v_refs, r_ref, out_refs, w_refs = refs[:2], refs[2], refs[3:5], refs[5:]
    cols, sites = p_ref.shape[2], p_ref.shape[3]
    rows = v_refs[0].shape[2]
    for colour in range(p_ref.shape[1]):
        real = p_ref[0, colour].T
        imag = p_ref[1, colour].T
        r_ref[colour, :sites, :cols] = real
        r_ref[colour, :sites, cols:] = imag
        r_ref[colour, sites:, :cols] = -imag
        r_ref[colour, sites:, cols:] = real
    total, squares = project_rows(trivial, v_refs, tab_ref, lambda colour: r_ref[colour], w_refs)
    for k, out_ref in enumerate(out_refs):
        for g in range(len(trivial)):
            at = (2 * g + k) * rows
            for part in range(2):
                out_ref[2 * g + part] = total[at : at + rows, part * cols : (part + 1) * cols]
        out_ref[2 * len(trivial)] = square_tile(squares[k], k)


def slab_kernel(v_ref, *refs):
    slab_refs, own_refs = refs[:-2], refs[-2:]
    me = lax.axis_index("tm")
    for k, ref in enumerate(slab_refs, 1):
        ref[...] = v_ref[pl.ds(2 * jnp.bitwise_xor(lax.div(me, 2), k), 2)]
    for k, ref in enumerate(own_refs):
        ref[...] = v_ref[jnp.bitwise_xor(me, k)]


def part_kernel(core_ref, *refs):
    slab_refs, out_ref = refs[:-1], refs[-1]
    for n, slab_ref in enumerate(slab_refs):
        out_ref[n] = slab_ref[1 - core_ref[0]]


def sums_kernel(trivial, half, core_ref, tab_ref, r_ref, *refs):
    given = len(refs) - 1 - r_ref.shape[0]
    out_ref, w_refs = refs[given], refs[given + 1 :]
    count, tiles, rows, cols = out_ref.shape
    if half == 0:
        v_refs = [slab_ref.at[core_ref[0]] for slab_ref in refs[:given]]
    else:
        v_refs = [refs[0].at[n] for n in range(count)]
    total, squares = project_rows(trivial, v_refs, tab_ref, lambda colour: r_ref[colour], w_refs)
    for n in range(count):
        for g in range(len(trivial)):
            low = (g * count + n) * rows
            for part in range(2):
                out_ref[n, 2 * g + part] = total[low : low + rows, part * cols : (part + 1) * cols]
        out_ref[n, tiles - 1] = square_tile(squares[n], half)


def rows_kernel(trivial, order, where_ref, tab_ref, r_ref, *refs):
    own_ref, sibling_ref, stay_ref, came_ref, last_stay_ref, last_v_ref = refs[:6]
    owners = len(order) + 1
    early = stay_ref.shape[0]
    late = owners - 1 - early
    out_refs, acc_ref, w_refs = refs[6 : 6 + owners], refs[6 + owners], refs[7 + owners :]
    tiles, rows, cols = own_ref.shape
    v_refs = [last_v_ref.at[n] for n in range(late)]
    total, squares = project_rows(trivial, v_refs, tab_ref, lambda colour: r_ref[colour], w_refs)
    halves = [(0, [own_ref[n] for n in range(tiles)], [sibling_ref[n] for n in range(tiles)])]
    for n, k in enumerate(order[:early]):
        halves.append((k, [stay_ref[n, i] for i in range(tiles)], [came_ref[n, i] for i in range(tiles)]))
    for n, k in enumerate(order[early:]):
        right = [
            total[(g * late + n) * rows : (g * late + n + 1) * rows, part * cols : (part + 1) * cols]
            for g in range(len(trivial))
            for part in range(2)
        ]
        right.append(square_tile(squares[n], 1))
        halves.append((k, [last_stay_ref[n, i] for i in range(tiles)], right))
    for k, left, right in halves:
        for tile in range(tiles - 1):
            at = 2 * rows * tile
            acc_ref[k, at : at + rows] = left[tile]
            acc_ref[k, at + rows : at + 2 * rows] = right[tile]
        acc_ref[k, 2 * rows * (tiles - 1) :] = left[tiles - 1] + right[tiles - 1]
    for q, out_ref in enumerate(out_refs):
        out_ref[...] = acc_ref[jnp.bitwise_xor(where_ref[0], q)].astype(out_ref.dtype)


def add_kernel(*refs):
    total = refs[0][...]
    for ref in refs[1:-1]:
        total = total + ref[...].astype(jnp.float32)
    refs[-1][...] = total


def finish_kernel(group, core_ref, *refs):
    count = len(group)
    parts, out_ref = refs[:-1], refs[-1]
    groups = max(group) + 1
    rows = out_ref.shape[1] // 4
    last = 4 * rows * groups

    def summed(at, size):
        value = parts[0][at : at + size].astype(jnp.float32)
        for ref in parts[1:]:
            value = value + ref[at : at + size].astype(jnp.float32)
        return value

    both = jnp.broadcast_to(summed(last, rows)[:1], (2 * rows, LANES))
    lane = lax.broadcasted_iota(jnp.int32, both.shape, 1)
    place = lax.broadcasted_iota(jnp.int32, both.shape, 0)
    mine = (lane == place) | (lane == place + 2 * rows)
    squares = jnp.sum(jnp.where(mine, both, 0.0), axis=1, keepdims=True)
    inverse = lax.rsqrt(squares + epsilon_norm)
    for g in range(groups):
        for part in range(2):
            value = summed(2 * rows * (2 * g + part), 2 * rows) * inverse
            for other in range(2):
                first = pl.multiple_of(jnp.bitwise_xor(core_ref[0], other) * (2 * rows), 2 * rows)
                half = value[other * rows : (other + 1) * rows]
                for m in range(count):
                    if group[m] == g:
                        out_ref[m, pl.ds(first + part, rows, stride=2), :] = half


def in_vmem(count):
    return [pl.BlockSpec(memory_space=pltpu.VMEM)] * count


def scalar():
    return [pl.BlockSpec(memory_space=pltpu.SMEM)]


def per_device_permutes(eigen_vectors, propagators):
    tm, space = lax.axis_size("tm"), lax.axis_size("space")
    me, z = lax.axis_index("tm"), lax.axis_index("space")
    rows, sites = eigen_vectors.shape[2], eigen_vectors.shape[4]
    cols = propagators.shape[2]
    waves, group = distinct_rows(window_waves(sites * space))
    groups = len(waves)
    trivial = tuple(not wave.any() for wave in waves)
    cosine, sine = trig_tables(waves)
    tables = np.stack([cosine, sine], 1).reshape(2 * groups, space, sites).transpose(1, 0, 2)
    table = lax.dynamic_index_in_dim(jnp.asarray(tables), z, 0, keepdims=False)

    vectors = jnp.transpose(eigen_vectors, (0, 1, 3, 2, 4))
    columns = jnp.transpose(propagators[0], (0, 2, 1, 3))
    colours = vectors.shape[2]

    def swapped(mine, r):
        return lax.ppermute(mine, "tm", [(i, i ^ r) for i in range(tm)])

    tiles = 2 * groups + 1
    tile = lambda dtype: jax.ShapeDtypeStruct((tiles, rows, cols), dtype)
    payload = lambda dtype: jax.ShapeDtypeStruct((2 * rows * (tiles - 1) + rows, cols), dtype)
    w_scratch = lambda count: [pltpu.VMEM((groups * count * rows, 2 * sites), jnp.bfloat16)] * colours
    small = pl.CostEstimate(flops=0, bytes_accessed=0, transcendentals=0)
    params = pltpu.CompilerParams(vmem_limit_bytes=12 * 2**20)

    one = lambda *lead: jax.ShapeDtypeStruct(lead + vectors.shape[1:], vectors.dtype)
    *slabs, own, sibling = pl.pallas_call(
        slab_kernel,
        out_shape=[one(2)] * (space - 1) + [one()] * 2,
        in_specs=in_vmem(1),
        out_specs=in_vmem(space + 1),
        cost_estimate=small,
        compiler_params=params,
    )(vectors)
    order, cut = (2, 1, 3), 2
    slabs = [swapped(slabs[k - 1], 2 * k) for k in order]
    sibling = swapped(sibling, 1)

    right, own_sums, sibling_sums = pl.pallas_call(
        functools.partial(first_kernel, trivial),
        out_shape=[jax.ShapeDtypeStruct((colours, 2 * sites, 2 * cols), jnp.bfloat16)]
        + [tile(jnp.float32)] * 2,
        in_specs=in_vmem(4),
        out_specs=in_vmem(3),
        scratch_shapes=w_scratch(2),
        cost_estimate=small,
        compiler_params=params,
    )(table, columns, own, sibling)

    where = jnp.bitwise_xor(me // 2, z).astype(jnp.int32).reshape(1)
    core = (me % 2).astype(jnp.int32).reshape(1)
    def part_of(slabs):
        leaving = pl.pallas_call(
            part_kernel,
            out_shape=one(len(slabs)),
            in_specs=scalar() + in_vmem(len(slabs)),
            out_specs=in_vmem(1)[0],
            cost_estimate=small,
            compiler_params=params,
        )(core, *slabs)
        return swapped(leaving, 1)

    def sums_of(half, count, *pieces):
        return pl.pallas_call(
            functools.partial(sums_kernel, trivial, half),
            out_shape=jax.ShapeDtypeStruct((count, tiles, rows, cols), jnp.float32),
            in_specs=scalar() + in_vmem(2 + len(pieces)),
            out_specs=in_vmem(1)[0],
            scratch_shapes=w_scratch(count),
            cost_estimate=small,
            compiler_params=params,
        )(core, table, right, *pieces)

    own_sums, early = lax.optimization_barrier((own_sums, slabs[:cut]))
    stay_sums = sums_of(0, len(early), *early)
    came_sums = sums_of(1, len(early), part_of(early))
    stay_sums, late = lax.optimization_barrier((stay_sums, slabs[cut:]))
    last_sums = sums_of(0, len(late), *late)
    own, *others = pl.pallas_call(
        functools.partial(rows_kernel, trivial, order),
        out_shape=[payload(jnp.float32)] + [payload(jnp.bfloat16)] * (space - 1),
        in_specs=scalar() + in_vmem(8),
        out_specs=in_vmem(space),
        scratch_shapes=[pltpu.VMEM((space,) + payload(jnp.float32).shape, jnp.float32)] + w_scratch(len(late)),
        cost_estimate=small,
        compiler_params=params,
    )(where, table, right, own_sums, sibling_sums, stay_sums, came_sums, last_sums, part_of(late))
    parts = [own]
    for q in (2, 3, 1):
        parts.append(lax.ppermute(others[q - 1], "space", [(i, i ^ q) for i in range(space)]))
    early_sum = pl.pallas_call(
        add_kernel,
        out_shape=payload(jnp.float32),
        in_specs=in_vmem(len(parts) - 1),
        out_specs=in_vmem(1)[0],
        cost_estimate=small,
        compiler_params=params,
    )(*parts[:-1])
    parts = [early_sum, parts[-1]]
    out = pl.pallas_call(
        functools.partial(finish_kernel, group),
        out_shape=jax.ShapeDtypeStruct((len(group), 2 * rows * 2, cols), jnp.float32),
        in_specs=scalar() + in_vmem(len(parts)),
        out_specs=in_vmem(1)[0],
        cost_estimate=small,
        compiler_params=params,
    )(core, *parts)
    return out.reshape(len(group), 2 * rows, 1, 2, cols)


def project(vectors, columns, cosine, sine):
    slices = vectors.shape[0]
    real_in = vectors[:, 0].astype(jnp.float32)
    imag_in = vectors[:, 1].astype(jnp.float32)
    w_real = (cosine * real_in - sine * imag_in).astype(jnp.bfloat16)
    w_imag = (-(sine * real_in + cosine * imag_in)).astype(jnp.bfloat16)
    left = jnp.stack([w_real, w_imag], 1)
    left = left.reshape(slices, 2, left.shape[2], -1)
    right = columns.reshape(slices, 2, columns.shape[2], -1)
    products = jnp.einsum("tcek,tdak->etcda", left, right, preferred_element_type=jnp.float32)
    real_out = products[:, :, 0, 0] - products[:, :, 1, 1]
    imag_out = products[:, :, 0, 1] + products[:, :, 1, 0]
    return jnp.stack([real_out, imag_out], 2)


def per_device_general(eigen_vectors, propagators):
    vectors = lax.all_to_all(eigen_vectors, "tm", split_axis=0, concat_axis=2, tiled=True)
    sites = vectors.shape[4]
    space = lax.axis_size("space")
    rows = vectors.shape[2] // space
    z = lax.axis_index("space")
    squares = lax.psum(jnp.sum(jnp.square(vectors.astype(jnp.float32)), axis=(1, 3, 4)), "space")
    inverse = lax.rsqrt(squares + epsilon_norm)
    mine = lax.dynamic_slice_in_dim(inverse, z * rows, rows, 1)
    row_scale = jnp.transpose(mine)[:, :, None, None]
    waves, group = distinct_rows(window_waves(sites * space))
    positions = z * sites + jnp.arange(sites, dtype=jnp.int32)
    coords = (positions // (LS * LS), positions // LS % LS, positions % LS)
    results = []
    for g in range(len(waves)):
        momentum = momenta_table[group.index(g)]
        wave = sum(n * x for n, x in zip(momentum, coords)) % LS
        angle = wave.astype(jnp.float32) * (2.0 * math.pi / LS)
        sums = project(vectors, propagators, jnp.cos(angle), jnp.sin(angle))
        sums = lax.psum_scatter(sums, "space", scatter_dimension=0, tiled=True)
        results.append(sums * row_scale)
    return jnp.stack([results[g] for g in group], 0)


def solution(mesh):
    tm, space = mesh.shape["tm"], mesh.shape["space"]

    def per_device(eigen_vectors, propagators):
        rows, sites = eigen_vectors.shape[2], eigen_vectors.shape[4]
        fits = (
            tm == 8
            and space == 4
            and eigen_vectors.shape[0] == tm
            and rows % 16 == 0
            and sites % LANES == 0
            and propagators.shape[2] == LANES
        )
        form = per_device_permutes if fits else per_device_general
        return form(eigen_vectors, propagators)

    placed = (P(None, None, "tm", None, "space"), P("tm", None, None, None, "space"))
    return jax.shard_map(
        per_device,
        mesh=mesh,
        in_specs=placed,
        out_specs=P(None, "space", "tm", None, None),
        check_vma=False,
    )
```
